32 devices in a mesh: group: 2 (over x), lat: 16 (over z, y, core).
Axes of the slice: x: 2, y: 2, z: 4, core: 2. Of those that a mesh axis runs over, the one named last changes fastest.
Arguments:
- inputs: bfloat16 [64, 1440, 256], P(('group', 'lat')), parts along dimension 0, may hold values from -6 to 6
- cotangent: bfloat16 [64, 1440, 256], P(('group', 'lat')), parts along dimension 0, may hold values from -6 to 6
- weight: bfloat16 [9, 256, 256], replicated, may hold values from -0.125 to 0.125
- pat_rows: int32 [32, 9, 3], replicated, may hold values from -2 to 2, as said below
- pat_lons: int32 [32, 9, 3], replicated, may hold values from -12 to 12, as said below
- pat_vals: float32 [32, 9, 3], replicated, may hold values from 0.05 to 0.35
Outputs:
- mixed: bfloat16 [64, 1440, 256], P(('group', 'lat')), parts along dimension 0
- grad_input: bfloat16 [64, 1440, 256], P(('group', 'lat')), parts along dimension 0
- grad_weight: float32 [18, 256, 256], P('group'), parts along dimension 0
The draws below stay inside these ranges and needn't reach their ends.
There are 2 independent parts, one for each index of `group`. The reference program is written for one: setup_inputs(seed, part) draws one part's arguments, and reference() takes and returns one part's arrays. A program takes and returns all parts, laid end to end along the dimension named above; an argument that names none is the same for every part. Nothing has to cross between parts.
Inputs may be any that keep to these rules, and one draw needn't show every extreme that they name: Every source row i + pat_rows lies in the grid. `pat_lons`: rows near either end of the grid reach farther in longitude.
All inputs are finite; a program needn't handle non-finite values.
Results may differ from the reference program's by a relative error of at most 0.005.
Values may be sent and summed in bfloat16 or wider, within the bound.
No kernel may reach another device: no remote copies, remote signals or barrier semaphores. Data moves between devices by JAX's collectives and lax.ppermute only.
A program may use at most 128 MiB of HBM per device.

```python
import math
import jax
import jax.numpy as jnp
from jax import lax

C = 256
NLON = 1440
K = 9
EP = 3
H = 2
LMAX = 12
NLAT = 32


def draw_pat_rows(key, part):
    key = jax.random.fold_in(key, 11)
    line = jnp.arange(NLAT, dtype=jnp.int32)[:, None, None]
    offsets = jax.random.randint(key, (NLAT, K, EP), -H, H + 1, dtype=jnp.int32)
    offsets = jnp.clip(offsets, -line, NLAT - 1 - line)
    offsets = offsets.at[NLAT // 2, 0, 0].set(H)
    offsets = offsets.at[NLAT // 2, 0, 1].set(-H)
    return offsets.astype(jnp.int32)


def draw_pat_lons(key, part):
    key = jax.random.fold_in(key, 23)
    line = jnp.arange(NLAT, dtype=jnp.int32)[:, None, None]
    edge = jnp.minimum(line, NLAT - 1 - line)
    reach = jnp.maximum(1, LMAX - edge * LMAX * 4 // NLAT)
    bits = jax.random.randint(key, (NLAT, K, EP), 0, 1048576, dtype=jnp.int32)
    offsets = bits % (2 * reach + 1) - reach
    offsets = offsets.at[0, 0, 0].set(LMAX)
    offsets = offsets.at[0, 0, 1].set(-LMAX)
    return offsets.astype(jnp.int32)


def steps_of(key, shape, cuts, low, high):
    def one(position, parts):
        draws = jax.random.uniform(jax.random.fold_in(jax.random.fold_in(key, 6), position), (parts,), jnp.float32, low / len(cuts), high / len(cuts))
        return jnp.repeat(jnp.exp(draws), shape[position] // parts).reshape((-1,) + (1,) * (len(shape) - position - 1))

    factor_of = one(*cuts[0])
    for cut in cuts[1:]:
        factor_of = factor_of * one(*cut)
    return factor_of


def gaussian(own_key, shape, deviation, most, cuts=(), kind=jnp.bfloat16):
    values = jax.random.normal(own_key, shape, jnp.float32) * deviation
    if len(cuts) > 0:
        values = steps_of(own_key, shape, cuts, -0.22, 0.18) * values
    return jnp.clip(values, min=-most, max=most).astype(kind)


def setup_inputs(seed: int = 0, part: int = 0) -> dict:
    streams_of = jax.random.split(jax.random.key(seed), 7)
    part_splits = jax.random.split(jax.random.fold_in(streams_of[6], part), 7)
    inputs = gaussian(part_splits[0], (NLAT, NLON, C), 1.0, 6.0, ((0, 16),))
    cotangent = gaussian(part_splits[1], (NLAT, NLON, C), 1.0, 6.0, ((0, 16),))
    weight = gaussian(streams_of[2], (K, C, C), (K * C) ** -0.5, 0.125)
    pat_rows = draw_pat_rows(jax.random.fold_in(streams_of[6], 71), part)
    pat_lons = draw_pat_lons(jax.random.fold_in(streams_of[6], 71), part)
    pat_vals = jnp.clip(jax.random.uniform(streams_of[5], (NLAT, K, EP), jnp.float32, 0.05, 0.35), 0.05, 0.35)
    return {"inputs": inputs, "cotangent": cotangent, "weight": weight, "pat_rows": pat_rows, "pat_lons": pat_lons, "pat_vals": pat_vals}


def reference(inputs, cotangent, weight, pat_rows, pat_lons, pat_vals):
    scale = 1.0 / math.sqrt(NLAT * NLON)
    cols = jnp.arange(NLON, dtype=jnp.int32)
    w_full = weight.astype(jnp.float32)

    def step(carry, items):
        grad, grad_w = carry
        row, drows, dlons, values, cot_row = items
        source = row + drows
        lon = (cols[None, None, :] + dlons[..., None]) % NLON
        picked = inputs[source[..., None], lon]
        basis = lax.optimization_barrier(jnp.sum(values[..., None, None] * picked.astype(jnp.float32), axis=1)).astype(jnp.bfloat16)
        basis_f = basis.astype(jnp.float32)
        cot_f = cot_row.astype(jnp.float32)
        out = jnp.einsum('kjc,kcd->jd', basis_f, w_full).astype(jnp.bfloat16)
        dbasis = jnp.einsum('jd,kcd->kjc', cot_f, w_full).astype(jnp.bfloat16)
        grad_w = grad_w + jnp.einsum('kjc,jd->kcd', basis_f, cot_f)
        terms = values[..., None, None] * dbasis[:, None].astype(jnp.float32)
        grad = grad.at[source[..., None], lon].add(terms)
        return ((grad, grad_w), out)
    init = (jnp.zeros((NLAT, NLON, C), jnp.float32), jnp.zeros((K, C, C), jnp.float32))
    rows = jnp.arange(NLAT, dtype=jnp.int32)
    (grad, grad_w), mixed = lax.scan(step, init, (rows, pat_rows, pat_lons, pat_vals, cotangent))
    return (mixed, grad.astype(jnp.bfloat16), grad_w * scale)
```

```python
import math

import jax
import jax.numpy as jnp
from jax import lax
from jax.experimental import pallas as pl
from jax.experimental.pallas import tpu as pltpu
from jax.sharding import PartitionSpec as P

H = 2
PAD = 16
GROUP = 4


def fwd_kernel(prow, plon, pval, own, above, below, cot, weight, mixed, gw, xf, basis, cott):
    rows, width, chan = own.shape
    nk = weight.shape[0]
    ne = prow.shape[0] // (rows * nk)
    half = 128
    nh = chan // half

    def widen(src, r, dst):
        for h in range(nh):
            cols = slice(h * half, (h + 1) * half)
            xf[dst, h, PAD : PAD + width] = src[r, :, cols].astype(jnp.float32)
            xf[dst, h, 0:PAD] = src[r, width - PAD : width, cols].astype(jnp.float32)
            xf[dst, h, PAD + width :] = src[r, 0:PAD, cols].astype(jnp.float32)

    for r in range(H):
        widen(above, r, r)
        widen(below, r, H + rows + r)
    for r in range(rows):
        widen(own, r, H + r)
    wall = weight[...].reshape(nk * chan, chan)
    for i in range(rows):
        cott[...] = cot[i].T

        def per_k(k, carry):
            vs = [pval[(i * nk + k) * ne + e] for e in range(ne)]
            rs = [i + H + prow[(i * nk + k) * ne + e] for e in range(ne)]
            os = [PAD + plon[(i * nk + k) * ne + e] for e in range(ne)]
            for h in range(nh):
                t = vs[0] * xf[rs[0], h, pl.ds(os[0], width), :]
                for e in range(1, ne):
                    t = t + vs[e] * xf[rs[e], h, pl.ds(os[e], width), :]
                basis[k, :, h * half : (h + 1) * half] = t.astype(jnp.bfloat16)
            return carry

        lax.fori_loop(0, nk, per_k, 0)
        tile = width // 3
        for t in range(3):
            sl = slice(t * tile, (t + 1) * tile)
            acc = jnp.dot(basis[0, sl], weight[0], preferred_element_type=jnp.float32)
            for k in range(1, nk):
                acc = acc + jnp.dot(basis[k, sl], weight[k], preferred_element_type=jnp.float32)
            mixed[i, sl] = acc.astype(jnp.bfloat16)
        for k in range(nk):
            p = jnp.dot(cott[...], basis[k], preferred_element_type=jnp.float32)
            if i == 0:
                gw[k] = p
            else:
                gw[k] = gw[k] + p
    for k in range(nk):
        gw[k] = gw[k].T


def forward(prow, plon, pval, own, above, below, cot, weight):
    rows, width, chan = own.shape
    nk = weight.shape[0]
    smem = pl.BlockSpec(memory_space=pltpu.SMEM)
    vmem = pl.BlockSpec(memory_space=pltpu.VMEM)
    return pl.pallas_call(
        fwd_kernel,
        in_specs=[smem] * 3 + [vmem] * 5,
        out_specs=[vmem] * 2,
        out_shape=[
            jax.ShapeDtypeStruct((rows, width, chan), jnp.bfloat16),
            jax.ShapeDtypeStruct((nk, chan, chan), jnp.float32),
        ],
        scratch_shapes=[
            pltpu.VMEM((rows + 2 * H, chan // 128, width + 2 * PAD, 128), jnp.float32),
            pltpu.VMEM((nk, width, chan), jnp.bfloat16),
            pltpu.VMEM((chan, width), jnp.bfloat16),
        ],
        compiler_params=pltpu.CompilerParams(vmem_limit_bytes=56 * 2**20),
        name="forward",
    )(prow, plon, pval, own, above, below, cot, weight)


def bwd_kernel(prow, plon, pval, cot, weight, own, above, below, db, acc, cnt, lst_n, lst_o, lst_v):
    rows, width, chan = cot.shape
    nk = weight.shape[0]
    ne = prow.shape[0] // (rows * nk)
    half = 128
    nh = chan // half
    lines = rows + 2 * H
    cap = rows * nk * ne + GROUP

    for t in range(lines):
        cnt[t] = 0

    def bin_one(n, carry):
        i = n // nk
        k = n - i * nk
        for e in range(ne):
            t = i + H + prow[(i * nk + k) * ne + e]
            c = cnt[t]
            lst_n[t * cap + c] = n
            lst_o[t * cap + c] = PAD - plon[(i * nk + k) * ne + e]
            lst_v[t * cap + c] = pval[(i * nk + k) * ne + e]
            cnt[t] = c + 1
        return carry

    lax.fori_loop(0, rows * nk, bin_one, 0)
    for t in range(lines):
        c = cnt[t]
        for g in range(GROUP - 1):
            lst_n[t * cap + c + g] = 0
            lst_o[t * cap + c + g] = PAD
            lst_v[t * cap + c + g] = 0.0

    for i in range(rows):
        def per_k(k, carry):
            n = i * nk + k
            d = lax.dot_general(cot[i], weight[k], (((1,), (1,)), ((), ())), preferred_element_type=jnp.float32)
            for h in range(nh):
                cols = slice(h * half, (h + 1) * half)
                db[n, h, PAD : PAD + width] = d[:, cols]
                db[n, h, 0:PAD] = d[width - PAD :, cols]
                db[n, h, PAD + width :] = d[0:PAD, cols]
            return carry

        lax.fori_loop(0, nk, per_k, 0)

    for t in range(lines):
        for h in range(nh):
            acc[h] = jnp.zeros((width, half), jnp.float32)

        def group(g, carry):
            at = t * cap + g * GROUP
            ns = [lst_n[at + j] for j in range(GROUP)]
            os = [lst_o[at + j] for j in range(GROUP)]
            vs = [lst_v[at + j] for j in range(GROUP)]
            for h in range(nh):
                s = vs[0] * db[ns[0], h, pl.ds(os[0], width), :]
                for j in range(1, GROUP):
                    s = s + vs[j] * db[ns[j], h, pl.ds(os[j], width), :]
                acc[h] = acc[h] + s
            return carry

        lax.fori_loop(0, (cnt[t] + GROUP - 1) // GROUP, group, 0)
        dst = above if t < H else (own if t < H + rows else below)
        r = t if t < H else (t - H if t < H + rows else t - H - rows)
        for h in range(nh):
            dst[r, :, h * half : (h + 1) * half] = acc[h].astype(dst.dtype)


def backward(prow, plon, pval, cot, weight):
    rows, width, chan = cot.shape
    nk = weight.shape[0]
    ne = prow.shape[0] // (rows * nk)
    smem = pl.BlockSpec(memory_space=pltpu.SMEM)
    vmem = pl.BlockSpec(memory_space=pltpu.VMEM)
    lines = rows + 2 * H
    cap = rows * nk * ne + GROUP
    return pl.pallas_call(
        bwd_kernel,
        in_specs=[smem] * 3 + [vmem] * 2,
        out_specs=[vmem] * 3,
        out_shape=[
            jax.ShapeDtypeStruct((rows, width, chan), jnp.float32),
            jax.ShapeDtypeStruct((H, width, chan), jnp.bfloat16),
            jax.ShapeDtypeStruct((H, width, chan), jnp.bfloat16),
        ],
        scratch_shapes=[
            pltpu.VMEM((rows * nk, chan // 128, width + 2 * PAD, 128), jnp.float32),
            pltpu.VMEM((chan // 128, width, 128), jnp.float32),
            pltpu.SMEM((lines,), jnp.int32),
            pltpu.SMEM((lines * cap,), jnp.int32),
            pltpu.SMEM((lines * cap,), jnp.int32),
            pltpu.SMEM((lines * cap,), jnp.float32),
        ],
        compiler_params=pltpu.CompilerParams(vmem_limit_bytes=56 * 2**20),
        name="backward",
    )(prow, plon, pval, cot, weight)


def sum_over_lat(value):
    size = lax.axis_size("lat")
    shape = value.shape
    value = value.reshape(-1, shape[-1])
    if size & (size - 1) or value.shape[0] % size:
        return lax.psum(value, "lat").reshape(shape)
    index = lax.axis_index("lat")
    bits = [1 << b for b in range(size.bit_length() - 1)]
    for bit in bits:
        side = (index // bit) % 2
        count = value.shape[0] // 2
        keep = lax.dynamic_slice_in_dim(value, side * count, count, 0)
        send = lax.dynamic_slice_in_dim(value, (1 - side) * count, count, 0).astype(jnp.bfloat16)
        got = lax.ppermute(send, "lat", [(i, i ^ bit) for i in range(size)])
        value = keep + got.astype(jnp.float32)
    value = value.astype(jnp.bfloat16)
    for bit in reversed(bits):
        side = (index // bit) % 2
        got = lax.ppermute(value, "lat", [(i, i ^ bit) for i in range(size)])
        value = jnp.where(
            side == 0, jnp.concatenate([value, got]), jnp.concatenate([got, value])
        )
    return value.reshape(shape)


def per_device(inputs, cotangent, weight, pat_rows, pat_lons, pat_vals):
    rows = inputs.shape[0]
    width = inputs.shape[1]
    size = lax.axis_size("lat")
    up = [(i, i + 1) for i in range(size - 1)]
    down = [(i + 1, i) for i in range(size - 1)]
    first = lax.axis_index("lat") * rows
    pattern = [
        lax.dynamic_slice_in_dim(table, first, rows, 0).reshape(-1)
        for table in (pat_rows, pat_lons, pat_vals)
    ]
    above = lax.ppermute(inputs[rows - H :], "lat", up)
    below = lax.ppermute(inputs[:H], "lat", down)
    grad, to_above, to_below = backward(*pattern, cotangent, weight)
    from_above = lax.ppermute(to_below, "lat", up)
    from_below = lax.ppermute(to_above, "lat", down)
    above, below, to_below, to_above = lax.optimization_barrier((above, below, to_below, to_above))
    mixed, partial_w = forward(*pattern, inputs, above, below, cotangent, weight)
    total_w = sum_over_lat(partial_w)
    grad_weight = total_w.astype(jnp.float32) * (1.0 / math.sqrt(pat_rows.shape[0] * width))
    grad = grad.at[:H].add(from_above.astype(jnp.float32))
    grad = grad.at[rows - H :].add(from_below.astype(jnp.float32))
    return (mixed, grad.astype(jnp.bfloat16), grad_weight)


def solution(mesh):
    return jax.shard_map(
        per_device,
        mesh=mesh,
        in_specs=(
            P(("group", "lat"), None, None),
            P(("group", "lat"), None, None),
            P(),
            P(),
            P(),
            P(),
        ),
        out_specs=(
            P(("group", "lat"), None, None),
            P(("group", "lat"), None, None),
            P("group", None, None),
        ),
        check_vma=False,
    )
```

```python
import math

import jax
import jax.numpy as jnp
from jax import lax
from jax.experimental import pallas as pl
from jax.experimental.pallas import tpu as pltpu
from jax.sharding import PartitionSpec as P

H = 2
PAD = 16
GROUP = 4
HALF = 128


def entry(table, i, k, e, ne):
    return (
        table[i, k, e].astype(jnp.int32),
        table[i, k, ne + e].astype(jnp.int32),
        table[i, k, 2 * ne + e],
    )


def fwd_kernel(last, table, *refs):
    if last:
        own, slow, fast, cot, weight, earlier, mixed, keep, send, xf, basis, cott = refs
    else:
        own, slow, fast, cot, weight, mixed, keep, send, xf, basis, cott = refs
    rows, width, _ = own.shape
    chan = cot.shape[2]
    nk = weight.shape[0]
    ne = table.shape[2] // 3
    odd = table[0, 0, 3 * ne] > 0.5

    def widen(src, r, dst):
        def part(at, to):
            xf[dst, to] = src[r, at].astype(jnp.float32)

        part(slice(0, width), slice(PAD, PAD + width))
        part(slice(width - PAD, width), slice(0, PAD))
        part(slice(0, PAD), slice(PAD + width, 2 * PAD + width))

    for r in range(H):
        widen(slow, r, jnp.where(odd, H + rows, 0) + r)
        widen(fast, r, jnp.where(odd, 0, H + rows) + r)
    for r in range(rows):
        widen(own, r, H + r)
        cott[:, r * width : (r + 1) * width] = cot[r].T
    for i in range(rows):

        def per_k(k, carry):
            t = None
            for e in range(ne):
                line, lon, value = entry(table, i, k, e, ne)
                term = value * xf[i + H + line, pl.ds(PAD + lon, width), :]
                t = term if t is None else t + term
            cols = pl.ds(pl.multiple_of(k * HALF, HALF), HALF)
            basis[i * width : (i + 1) * width, cols] = t.astype(jnp.bfloat16)
            return carry

        lax.fori_loop(0, nk, per_k, 0)
    wflat = weight[...].reshape(nk * HALF, chan)
    parts = 3 * rows
    tile = rows * width // parts
    for p in range(parts):
        i, at = divmod(p * tile, width)
        acc = jnp.dot(basis[p * tile : (p + 1) * tile], wflat, preferred_element_type=jnp.float32)
        if last:
            mixed[i, at : at + tile] = (earlier[i, at : at + tile] + acc).astype(jnp.bfloat16)
        else:
            mixed[i, at : at + tile] = acc
    gwt = jnp.dot(cott[...], basis[...], preferred_element_type=jnp.float32)
    dhalf = chan // 2
    for k in range(nk):
        mat = gwt[:, k * HALF : (k + 1) * HALF].T
        low, high = mat[:, :dhalf], mat[:, dhalf:]
        keep[k] = jnp.where(odd, high, low)
        send[k] = jnp.where(odd, low, high).astype(jnp.bfloat16)


def forward(table, own, slow, fast, cot, weight, h, earlier=None):
    rows, width, chan = cot.shape
    nk = weight.shape[0]
    smem = pl.BlockSpec(memory_space=pltpu.SMEM)
    vmem = pl.BlockSpec(memory_space=pltpu.VMEM)
    last = earlier is not None
    half = pl.BlockSpec((rows, width, HALF), lambda g: (0, 0, h))
    side = pl.BlockSpec((H, width, HALF), lambda g: (0, 0, h))
    wide = pl.BlockSpec((rows, width, chan), lambda g: (0, 0, 0))
    edge = pl.BlockSpec((H, width, HALF), lambda g: (0, 0, 0))
    part = pl.BlockSpec((nk, HALF, chan // 2), lambda g: (0, 0, 0))
    return pl.pallas_call(
        lambda *refs: fwd_kernel(last, *refs),
        grid=(1,),
        in_specs=[smem]
        + [half, edge, side, wide, pl.BlockSpec((nk, HALF, chan), lambda g: (0, h, 0))]
        + [wide] * last,
        out_specs=[wide, part, part],
        out_shape=[
            jax.ShapeDtypeStruct((rows, width, chan), jnp.bfloat16 if last else jnp.float32),
            jax.ShapeDtypeStruct((nk, HALF, chan // 2), jnp.float32),
            jax.ShapeDtypeStruct((nk, HALF, chan // 2), jnp.bfloat16),
        ],
        scratch_shapes=[
            pltpu.VMEM((rows + 2 * H, width + 2 * PAD, HALF), jnp.float32),
            pltpu.VMEM((rows * width, nk * HALF), jnp.bfloat16),
            pltpu.VMEM((chan, rows * width), jnp.bfloat16),
        ],
        compiler_params=pltpu.CompilerParams(vmem_limit_bytes=48 * 2**20),
        cost_estimate=pl.CostEstimate(
            flops=0, bytes_accessed=0, transcendentals=0
        ),
        name="forward",
    )(table, own, slow, fast, cot, weight, *([earlier] if last else []))


def bwd_kernel(table, cin, win, own, *rest):
    edges, scratch = rest[:2], rest[2:]
    db, acc, narrow, cnt, lst_n, lst_o, lst_v, out_sems = scratch
    rows, width, chan = cin.shape
    nk = win.shape[0]
    ne = table.shape[2] // 3
    odd = table[0, 0, 3 * ne] > 0.5
    nh = chan // HALF
    lines = rows + 2 * H
    cap = rows * nk * ne + GROUP
    for line in range(lines):
        cnt[line] = 0

    for i in range(rows):

        def bin_one(k, carry):
            for e in range(ne):
                row, lon, value = entry(table, i, k, e, ne)
                line = i + H + row
                c = cnt[line]
                lst_n[line * cap + c] = i * nk + k
                lst_o[line * cap + c] = PAD - lon
                lst_v[line * cap + c] = value
                cnt[line] = c + 1
            return carry

        lax.fori_loop(0, nk, bin_one, 0)
    for line in range(lines):
        c = cnt[line]
        for g in range(GROUP):
            lst_n[line * cap + c + g] = 0
            lst_o[line * cap + c + g] = PAD
            lst_v[line * cap + c + g] = 0.0
    for i in range(rows):
        for k in range(nk):
            n = i * nk + k
            d = lax.dot_general(
                cin[i], win[k], (((1,), (1,)), ((), ())), preferred_element_type=jnp.float32
            )
            for h in range(nh):
                cols = slice(h * HALF, (h + 1) * HALF)
                db[n, h, PAD : PAD + width] = d[:, cols]
                db[n, h, 0:PAD] = d[width - PAD :, cols]
                db[n, h, PAD + width :] = d[0:PAD, cols]

    def terms(t, g, h):
        s = None
        for j in range(GROUP):
            at = t * cap + g * GROUP + j
            x = lst_v[at] * db[lst_n[at], h, pl.ds(lst_o[at], width), :]
            s = x if s is None else s + x
        return s

    def line_sum(t, slot):
        for h in range(nh):
            acc[slot, :, h * HALF : (h + 1) * HALF] = terms(t, 0, h)

        def group(g, carry):
            for h in range(nh):
                cols = slice(h * HALF, (h + 1) * HALF)
                acc[slot, :, cols] = acc[slot, :, cols] + terms(t, g, h)
            return carry

        lax.fori_loop(1, (cnt[t] + GROUP - 1) // GROUP, group, 0)

    def edge(s, carry):
        top = (s < H) != odd
        line_sum(jnp.where(top, 0, H + rows) + s % H, rows)
        narrow[s] = acc[rows].astype(narrow.dtype)
        return carry

    lax.fori_loop(0, 2 * H, edge, 0)
    writes = [
        pltpu.make_async_copy(narrow.at[0:H], edges[0], out_sems.at[0]),
        pltpu.make_async_copy(narrow.at[H:], edges[1], out_sems.at[1]),
    ]
    writes.append(pltpu.make_async_copy(acc.at[0:rows], own, out_sems.at[2]))
    for write in writes[:2]:
        write.start()

    def inner(s, carry):
        line_sum(s + H, s)
        return carry

    lax.fori_loop(0, rows, inner, 0)
    writes[2].start()
    for write in writes:
        write.wait()


def backward(table, cot, weight):
    rows, width, chan = cot.shape
    nk = weight.shape[0]
    ne = table.shape[2] // 3
    smem = pl.BlockSpec(memory_space=pltpu.SMEM)
    anym = pl.BlockSpec(memory_space=pl.ANY)
    lines = rows + 2 * H
    cap = rows * nk * ne + GROUP
    return pl.pallas_call(
        bwd_kernel,
        in_specs=[smem] + [pl.BlockSpec(memory_space=pltpu.VMEM)] * 2,
        out_specs=[anym] * 3,
        out_shape=[
            jax.ShapeDtypeStruct((rows, width, chan), jnp.float32),
        ]
        + [jax.ShapeDtypeStruct((H, width, chan), jnp.bfloat16)] * 2,
        scratch_shapes=[
            pltpu.VMEM((rows * nk, chan // HALF, width + 2 * PAD, HALF), jnp.float32),
            pltpu.VMEM((rows + 1, width, chan), jnp.float32),
            pltpu.VMEM((2 * H, width, chan), jnp.bfloat16),
            pltpu.SMEM((lines,), jnp.int32),
            pltpu.SMEM((lines * cap,), jnp.int32),
            pltpu.SMEM((lines * cap,), jnp.int32),
            pltpu.SMEM((lines * cap,), jnp.float32),
            pltpu.SemaphoreType.DMA((3,)),
        ],
        compiler_params=pltpu.CompilerParams(vmem_limit_bytes=56 * 2**20),
        cost_estimate=pl.CostEstimate(
            flops=2 * rows * width * nk * chan * chan, bytes_accessed=12 * 2**20, transcendentals=0
        ),
        name="backward",
    )(table, cot, weight)


def swap(value, bit, size):
    return lax.ppermute(value, "lat", [(i, i ^ bit) for i in range(size)])


def sums_over_lat(keeps, sends, between):
    size = lax.axis_size("lat")
    shape = keeps[0].shape
    index = lax.axis_index("lat")
    values = []
    for keep, send in zip(keeps, sends):
        got = swap(send.reshape(-1, shape[-1]), 1, size)
        values.append(keep.reshape(-1, shape[-1]) + got.astype(jnp.float32))
    bits = [1 << b for b in range(1, size.bit_length() - 1)]
    halved = bits[1:]
    for bit in halved:
        values = between(bit, values)
        side = (index // bit) % 2
        count = values[0].shape[0] // 2
        for j, value in enumerate(values):
            kept = lax.dynamic_slice_in_dim(value, side * count, count, 0)
            sent = lax.dynamic_slice_in_dim(value, (1 - side) * count, count, 0)
            got = swap(sent.astype(jnp.bfloat16), bit, size)
            values[j] = kept + got.astype(jnp.float32)
    for bit in bits[:1]:
        values = between(bit, values)
        for j, value in enumerate(values):
            sent = value.astype(jnp.bfloat16)
            values[j] = sent.astype(jnp.float32) + swap(sent, bit, size).astype(jnp.float32)
    values = [value.astype(jnp.bfloat16) for value in values]
    for bit in reversed(halved):
        values = between(-bit, values)
        side = (index // bit) % 2
        for j, value in enumerate(values):
            got = swap(value, bit, size)
            values[j] = jnp.where(
                side == 0, jnp.concatenate([value, got]), jnp.concatenate([got, value])
            )
    for j, value in enumerate(values):
        got = swap(value, 1, size)
        first = jnp.where(index % 2 == 0, value, got)
        second = jnp.where(index % 2 == 0, got, value)
        values[j] = jnp.concatenate([first.reshape(shape), second.reshape(shape)], axis=-1)
    return values


def per_device(inputs, cotangent, weight, pat_rows, pat_lons, pat_vals):
    rows = inputs.shape[0]
    width = inputs.shape[1]
    size = lax.axis_size("lat")
    index = lax.axis_index("lat")
    odd = index % 2 == 1
    fast_pairs = [(i, i ^ 1) for i in range(size)]
    slow_pairs = [(i, i + 1 if i % 2 else i - 1) for i in range(1, size - 1)]
    near_pairs = [pair for pair in slow_pairs if min(pair) % 4 == 1]
    far_pairs = [pair for pair in slow_pairs if min(pair) % 4 == 3]
    if rows == H:
        to_slow = to_fast = inputs
    else:
        head, tail = inputs[:H], inputs[rows - H :]
        to_slow, to_fast = jnp.where(odd, tail, head), jnp.where(odd, head, tail)
    slow = [
        lax.ppermute(to_slow[:, :, h * HALF : (h + 1) * HALF], "lat", slow_pairs) for h in range(2)
    ]
    fast = lax.ppermute(to_fast, "lat", fast_pairs)
    side = jnp.full((rows, pat_rows.shape[1], 1), odd, jnp.float32)
    table = [
        lax.dynamic_slice_in_dim(part, index * rows, rows, 0).astype(jnp.float32)
        for part in (pat_rows, pat_lons, pat_vals)
    ]
    table = jnp.concatenate([*table, side], axis=-1)
    grad, edge_slow, edge_fast = backward(table, cotangent, weight)
    slow[0], fast, edge_slow, edge_fast = lax.optimization_barrier(
        (slow[0], fast, edge_slow, edge_fast)
    )
    mixed, keep0, send0 = forward(table, inputs, slow[0], fast, cotangent, weight, 0)
    mixed, edge_slow, edge_fast = lax.optimization_barrier((mixed, edge_slow, edge_fast))
    got_far = lax.ppermute(edge_slow, "lat", far_pairs)
    got_near = lax.ppermute(edge_slow, "lat", near_pairs)
    got_fast = lax.ppermute(edge_fast, "lat", fast_pairs)
    mixed, keep1, send1 = forward(table, inputs, slow[1], fast, cotangent, weight, 1, mixed)
    scale = 1.0 / math.sqrt(pat_rows.shape[0] * width)
    waits = {4: 0, 2: 1}
    got = [got_far, got_near]

    def between(bit, values):
        if bit in waits:
            at = waits[bit]
            values, got[at] = lax.optimization_barrier((values, got[at]))
        return list(values)

    sums = sums_over_lat([keep0, keep1], [send0, send1], between)
    grad_weight = jnp.concatenate(sums, axis=1).astype(jnp.float32) * scale
    from_slow = got[0].astype(jnp.float32) + got[1].astype(jnp.float32)
    from_fast = got_fast.astype(jnp.float32)
    if rows == H:
        grad = grad + from_slow + from_fast
    else:
        grad = grad.at[:H].add(jnp.where(odd, from_fast, from_slow))
        grad = grad.at[rows - H :].add(jnp.where(odd, from_slow, from_fast))
    return (mixed, grad.astype(jnp.bfloat16), grad_weight)


def solution(mesh):
    return jax.shard_map(
        per_device,
        mesh=mesh,
        in_specs=(
            P(("group", "lat"), None, None),
            P(("group", "lat"), None, None),
            P(),
            P(),
            P(),
            P(),
        ),
        out_specs=(
            P(("group", "lat"), None, None),
            P(("group", "lat"), None, None),
            P("group", None, None),
        ),
        check_vma=False,
    )
```

```python
import math

import jax
import jax.numpy as jnp
from jax import lax
from jax.experimental import pallas as pl
from jax.experimental.pallas import tpu as pltpu
from jax.sharding import PartitionSpec as P

H = 2
PAD = 16
GROUP = 4
HALF = 128


def entry(table, i, k, e, ne):
    return (
        table[i, k, e].astype(jnp.int32),
        table[i, k, ne + e].astype(jnp.int32),
        table[i, k, 2 * ne + e],
    )


def fwd_kernel(last, table, *refs):
    if last:
        own, slow, fast, cot, weight, earlier, keep_in, send_in, mixed, keep, send, xf, basis, cott = refs
    else:
        own, slow, fast, cot, weight, mixed, keep, send, xf, basis, cott = refs
    rows, width, _ = own.shape
    chan = cot.shape[2]
    nk = weight.shape[0]
    ne = table.shape[2] // 3
    odd = table[0, 0, 3 * ne] > 0.5

    def widen(src, r, dst):
        def part(at, to):
            xf[dst, to] = src[r, at].astype(jnp.float32)

        part(slice(0, width), slice(PAD, PAD + width))
        part(slice(width - PAD, width), slice(0, PAD))
        part(slice(0, PAD), slice(PAD + width, 2 * PAD + width))

    for r in range(H):
        widen(slow, r, jnp.where(odd, H + rows, 0) + r)
        widen(fast, r, jnp.where(odd, 0, H + rows) + r)
    for r in range(rows):
        widen(own, r, H + r)
        cott[:, r * width : (r + 1) * width] = cot[r].T
    for i in range(rows):

        def per_k(k, carry):
            t = None
            for e in range(ne):
                line, lon, value = entry(table, i, k, e, ne)
                term = value * xf[i + H + line, pl.ds(PAD + lon, width), :]
                t = term if t is None else t + term
            cols = pl.ds(pl.multiple_of(k * HALF, HALF), HALF)
            basis[i * width : (i + 1) * width, cols] = t.astype(jnp.bfloat16)
            return carry

        lax.fori_loop(0, nk, per_k, 0)
    wflat = weight[...].reshape(nk * HALF, chan)
    parts = 3 * rows
    tile = rows * width // parts
    for p in range(parts):
        i, at = divmod(p * tile, width)
        acc = jnp.dot(basis[p * tile : (p + 1) * tile], wflat, preferred_element_type=jnp.float32)
        if last:
            mixed[i, at : at + tile] = (earlier[i, at : at + tile] + acc).astype(jnp.bfloat16)
        else:
            mixed[i, at : at + tile] = acc
    gwt = jnp.dot(cott[...], basis[...], preferred_element_type=jnp.float32)
    dhalf = chan // 2
    at = nk if last else 0
    if last:
        keep[0:nk] = keep_in[...]
        send[0:nk] = send_in[...]
    for k in range(nk):
        mat = gwt[:, k * HALF : (k + 1) * HALF].T
        low, high = mat[:, :dhalf], mat[:, dhalf:]
        keep[at + k] = jnp.where(odd, high, low)
        send[at + k] = jnp.where(odd, low, high).astype(jnp.bfloat16)


def forward(table, own, slow, fast, cot, weight, h, earlier=()):
    rows, width, chan = cot.shape
    nk = weight.shape[0]
    smem = pl.BlockSpec(memory_space=pltpu.SMEM)
    vmem = pl.BlockSpec(memory_space=pltpu.VMEM)
    last = len(earlier) > 0
    count = nk * (1 + last)
    half = pl.BlockSpec((rows, width, HALF), lambda g: (0, 0, h))
    side = pl.BlockSpec((H, width, HALF), lambda g: (0, 0, h))
    wide = pl.BlockSpec((rows, width, chan), lambda g: (0, 0, 0))
    edge = pl.BlockSpec((H, width, HALF), lambda g: (0, 0, 0))

    def part(blocks):
        return pl.BlockSpec((blocks, HALF, chan // 2), lambda g: (0, 0, 0))

    return pl.pallas_call(
        lambda *refs: fwd_kernel(last, *refs),
        grid=(1,),
        in_specs=[smem]
        + [half, edge, side, wide, pl.BlockSpec((nk, HALF, chan), lambda g: (0, h, 0))]
        + ([wide, part(nk), part(nk)] if last else []),
        out_specs=[wide, part(count), part(count)],
        out_shape=[
            jax.ShapeDtypeStruct((rows, width, chan), jnp.bfloat16 if last else jnp.float32),
            jax.ShapeDtypeStruct((count, HALF, chan // 2), jnp.float32),
            jax.ShapeDtypeStruct((count, HALF, chan // 2), jnp.bfloat16),
        ],
        scratch_shapes=[
            pltpu.VMEM((rows + 2 * H, width + 2 * PAD, HALF), jnp.float32),
            pltpu.VMEM((rows * width, nk * HALF), jnp.bfloat16),
            pltpu.VMEM((chan, rows * width), jnp.bfloat16),
        ],
        compiler_params=pltpu.CompilerParams(vmem_limit_bytes=48 * 2**20),
        cost_estimate=pl.CostEstimate(
            flops=0, bytes_accessed=0, transcendentals=0
        ),
        name="forward",
    )(table, own, slow, fast, cot, weight, *earlier)


def bwd_kernel(table, cin, win, own, *rest):
    edges, scratch = rest[:2], rest[2:]
    db, acc, narrow, cnt, lst_n, lst_o, lst_v, out_sems = scratch
    rows, width, chan = cin.shape
    nk = win.shape[0]
    ne = table.shape[2] // 3
    odd = table[0, 0, 3 * ne] > 0.5
    nh = chan // HALF
    lines = rows + 2 * H
    cap = rows * nk * ne + GROUP
    for line in range(lines):
        cnt[line] = 0

    for i in range(rows):

        def bin_one(k, carry):
            for e in range(ne):
                row, lon, value = entry(table, i, k, e, ne)
                line = i + H + row
                c = cnt[line]
                lst_n[line * cap + c] = i * nk + k
                lst_o[line * cap + c] = PAD - lon
                lst_v[line * cap + c] = value
                cnt[line] = c + 1
            return carry

        lax.fori_loop(0, nk, bin_one, 0)
    for line in range(lines):
        c = cnt[line]
        for g in range(GROUP):
            lst_n[line * cap + c + g] = 0
            lst_o[line * cap + c + g] = PAD
            lst_v[line * cap + c + g] = 0.0
    for i in range(rows):
        for k in range(nk):
            n = i * nk + k
            d = lax.dot_general(
                cin[i], win[k], (((1,), (1,)), ((), ())), preferred_element_type=jnp.float32
            )
            for h in range(nh):
                cols = slice(h * HALF, (h + 1) * HALF)
                db[n, h, PAD : PAD + width] = d[:, cols]
                db[n, h, 0:PAD] = d[width - PAD :, cols]
                db[n, h, PAD + width :] = d[0:PAD, cols]

    def terms(t, g, h):
        s = None
        for j in range(GROUP):
            at = t * cap + g * GROUP + j
            x = lst_v[at] * db[lst_n[at], h, pl.ds(lst_o[at], width), :]
            s = x if s is None else s + x
        return s

    def line_sum(t, slot):
        for h in range(nh):
            acc[slot, :, h * HALF : (h + 1) * HALF] = terms(t, 0, h)

        def group(g, carry):
            for h in range(nh):
                cols = slice(h * HALF, (h + 1) * HALF)
                acc[slot, :, cols] = acc[slot, :, cols] + terms(t, g, h)
            return carry

        lax.fori_loop(1, (cnt[t] + GROUP - 1) // GROUP, group, 0)

    def edge(s, carry):
        top = (s < H) != odd
        line_sum(jnp.where(top, 0, H + rows) + s % H, rows)
        narrow[s] = acc[rows].astype(narrow.dtype)
        return carry

    lax.fori_loop(0, 2 * H, edge, 0)
    writes = [
        pltpu.make_async_copy(narrow.at[0:H], edges[0], out_sems.at[0]),
        pltpu.make_async_copy(narrow.at[H:], edges[1], out_sems.at[1]),
    ]
    writes.append(pltpu.make_async_copy(acc.at[0:rows], own, out_sems.at[2]))
    for write in writes[:2]:
        write.start()

    def inner(s, carry):
        line_sum(s + H, s)
        return carry

    lax.fori_loop(0, rows, inner, 0)
    writes[2].start()
    for write in writes:
        write.wait()


def backward(table, cot, weight):
    rows, width, chan = cot.shape
    nk = weight.shape[0]
    ne = table.shape[2] // 3
    smem = pl.BlockSpec(memory_space=pltpu.SMEM)
    anym = pl.BlockSpec(memory_space=pl.ANY)
    lines = rows + 2 * H
    cap = rows * nk * ne + GROUP
    return pl.pallas_call(
        bwd_kernel,
        in_specs=[smem] + [pl.BlockSpec(memory_space=pltpu.VMEM)] * 2,
        out_specs=[anym] * 3,
        out_shape=[
            jax.ShapeDtypeStruct((rows, width, chan), jnp.float32),
        ]
        + [jax.ShapeDtypeStruct((H, width, chan), jnp.bfloat16)] * 2,
        scratch_shapes=[
            pltpu.VMEM((rows * nk, chan // HALF, width + 2 * PAD, HALF), jnp.float32),
            pltpu.VMEM((rows + 1, width, chan), jnp.float32),
            pltpu.VMEM((2 * H, width, chan), jnp.bfloat16),
            pltpu.SMEM((lines,), jnp.int32),
            pltpu.SMEM((lines * cap,), jnp.int32),
            pltpu.SMEM((lines * cap,), jnp.int32),
            pltpu.SMEM((lines * cap,), jnp.float32),
            pltpu.SemaphoreType.DMA((3,)),
        ],
        compiler_params=pltpu.CompilerParams(vmem_limit_bytes=56 * 2**20),
        cost_estimate=pl.CostEstimate(flops=0, bytes_accessed=0, transcendentals=0),
        name="backward",
    )(table, cot, weight)


WAITS = (-1, 3)
ADDED = 4
TIED = True


def swap(value, bit, size):
    return lax.ppermute(value, "lat", [(i, i ^ bit) for i in range(size)])


def sum_over_lat(keep, send, between):
    size = lax.axis_size("lat")
    shape = keep.shape
    index = lax.axis_index("lat")
    whole = keep.reshape(-1, shape[-1])
    whole = whole + swap(send.reshape(-1, shape[-1]), 1, size).astype(jnp.float32)
    (whole,) = between(-1, [whole])
    values = list(jnp.split(whole, 2))
    rest = [1 << b for b in range(1, size.bit_length() - 1)]
    orders = [rest[1:] + rest[:1], rest]
    for step in range(len(rest) - 1):
        values = between(step, values)
        for j in range(2):
            bit = orders[j][step]
            side = (index // bit) % 2
            count = values[j].shape[0] // 2
            kept = lax.dynamic_slice_in_dim(values[j], side * count, count, 0)
            sent = lax.dynamic_slice_in_dim(values[j], (1 - side) * count, count, 0)
            got = swap(sent.astype(jnp.bfloat16), bit, size)
            values[j] = kept + got.astype(jnp.float32)
    values = between(len(rest) - 1, values)
    for j in range(2):
        sent = values[j].astype(jnp.bfloat16)
        got = swap(sent, orders[j][-1], size)
        values[j] = (sent.astype(jnp.float32) + got.astype(jnp.float32)).astype(jnp.bfloat16)
    for step in reversed(range(len(rest) - 1)):
        values = between(2 * len(rest) - 2 - step, values)
        for j in range(2):
            bit = orders[j][step]
            side = (index // bit) % 2
            got = swap(values[j], bit, size)
            values[j] = jnp.where(
                side == 0,
                jnp.concatenate([values[j], got]),
                jnp.concatenate([got, values[j]]),
            )
    values = between(2 * len(rest) - 1, values)
    parts = []
    for value in values:
        got = swap(value, 1, size)
        first = jnp.where(index % 2 == 0, value, got)
        second = jnp.where(index % 2 == 0, got, value)
        part = (shape[0] // 2, *shape[1:])
        parts.append(jnp.concatenate([first.reshape(part), second.reshape(part)], axis=-1))
    return jnp.concatenate(parts, axis=1)


def per_device(inputs, cotangent, weight, pat_rows, pat_lons, pat_vals):
    rows = inputs.shape[0]
    width = inputs.shape[1]
    size = lax.axis_size("lat")
    index = lax.axis_index("lat")
    odd = index % 2 == 1
    fast_pairs = [(i, i ^ 1) for i in range(size)]
    slow_pairs = [(i, i + 1 if i % 2 else i - 1) for i in range(1, size - 1)]
    near_pairs = [pair for pair in slow_pairs if min(pair) % 4 == 1]
    far_pairs = [pair for pair in slow_pairs if min(pair) % 4 == 3]
    if rows == H:
        to_slow = to_fast = inputs
    else:
        head, tail = inputs[:H], inputs[rows - H :]
        to_slow, to_fast = jnp.where(odd, tail, head), jnp.where(odd, head, tail)
    part = to_slow[:, :, :HALF]
    slow = [lax.ppermute(part, "lat", slow_pairs)]
    rest, part = lax.optimization_barrier((to_slow, part))
    slow.append(lax.ppermute(rest[:, :, HALF:], "lat", slow_pairs))
    fast = lax.ppermute(to_fast, "lat", fast_pairs)
    side = jnp.full((rows, pat_rows.shape[1], 1), odd, jnp.float32)
    table = [
        lax.dynamic_slice_in_dim(part, index * rows, rows, 0).astype(jnp.float32)
        for part in (pat_rows, pat_lons, pat_vals)
    ]
    table = jnp.concatenate([*table, side], axis=-1)
    grad, edge_slow, edge_fast = backward(table, cotangent, weight)
    slow[0], fast, edge_slow, edge_fast = lax.optimization_barrier(
        (slow[0], fast, edge_slow, edge_fast)
    )
    partial, *earlier = forward(table, inputs, slow[0], fast, cotangent, weight, 0)
    partial, edge_slow, edge_fast = lax.optimization_barrier((partial, edge_slow, edge_fast))
    got_far = lax.ppermute(edge_slow, "lat", far_pairs)
    got_near = lax.ppermute(edge_slow, "lat", near_pairs)
    got_fast = lax.ppermute(edge_fast, "lat", fast_pairs)
    mixed, keep, send = forward(table, inputs, slow[1], fast, cotangent, weight, 1, (partial, *earlier))
    scale = 1.0 / math.sqrt(pat_rows.shape[0] * width)
    got = [got_far, got_near]

    def between(step, values):
        nonlocal grad
        for j in range(2):
            if step == WAITS[j]:
                values, got[j] = lax.optimization_barrier((values, got[j]))
        if step == ADDED:
            from_slow = got[0].astype(jnp.float32) + got[1].astype(jnp.float32)
            from_fast = got_fast.astype(jnp.float32)
            if rows == H:
                grad = grad + from_slow + from_fast
            else:
                grad = grad.at[:H].add(jnp.where(odd, from_fast, from_slow))
                grad = grad.at[rows - H :].add(jnp.where(odd, from_slow, from_fast))
            grad = grad.astype(jnp.bfloat16)
            if TIED:
                values, grad = lax.optimization_barrier((values, grad))
        return list(values)

    total = sum_over_lat(keep, send, between)
    return (mixed, grad, total.astype(jnp.float32) * scale)


def solution(mesh):
    return jax.shard_map(
        per_device,
        mesh=mesh,
        in_specs=(
            P(("group", "lat"), None, None),
            P(("group", "lat"), None, None),
            P(),
            P(),
            P(),
            P(),
        ),
        out_specs=(
            P(("group", "lat"), None, None),
            P(("group", "lat"), None, None),
            P("group", None, None),
        ),
        check_vma=False,
    )
```

```python
import math

import jax
import jax.numpy as jnp
from jax import lax
from jax.experimental import pallas as pl
from jax.experimental.pallas import tpu as pltpu
from jax.sharding import PartitionSpec as P

H = 2
PAD = 16
GROUP = 4
HALF = 128


def entry(table, i, k, e, ne):
    return (
        table[i, k, e].astype(jnp.int32),
        table[i, k, ne + e].astype(jnp.int32),
        table[i, k, 2 * ne + e],
    )


def fwd_kernel(last, table, *refs):
    if last:
        own, near, far, fast, cot, weight, earlier, keep_in, send_in, mixed, keep, send, xf, basis, cott = refs
    else:
        own, near, far, fast, cot, weight, mixed, keep, send, xf, basis, cott = refs
    rows, width, _ = own.shape
    chan = cot.shape[2]
    nk = weight.shape[0]
    ne = table.shape[2] // 3
    odd = table[0, 0, 3 * ne] > 0.5

    def widen(src, r, dst, more=None):
        def part(at, to):
            piece = src[r, at].astype(jnp.float32)
            if more is not None:
                piece = piece + more[r, at].astype(jnp.float32)
            xf[dst, to] = piece

        part(slice(0, width), slice(PAD, PAD + width))
        part(slice(width - PAD, width), slice(0, PAD))
        part(slice(0, PAD), slice(PAD + width, 2 * PAD + width))

    for r in range(H):
        widen(near, r, jnp.where(odd, H + rows, 0) + r, far)
        widen(fast, r, jnp.where(odd, 0, H + rows) + r)
    for r in range(rows):
        widen(own, r, H + r)
        cott[:, r * width : (r + 1) * width] = cot[r].T
    for i in range(rows):

        def per_k(k, carry):
            t = None
            for e in range(ne):
                line, lon, value = entry(table, i, k, e, ne)
                term = value * xf[i + H + line, pl.ds(PAD + lon, width), :]
                t = term if t is None else t + term
            cols = pl.ds(pl.multiple_of(k * HALF, HALF), HALF)
            basis[i * width : (i + 1) * width, cols] = t.astype(jnp.bfloat16)
            return carry

        lax.fori_loop(0, nk, per_k, 0)
    wflat = weight[...].reshape(nk * HALF, chan)
    parts = 3 * rows
    tile = rows * width // parts
    for p in range(parts):
        i, at = divmod(p * tile, width)
        acc = jnp.dot(basis[p * tile : (p + 1) * tile], wflat, preferred_element_type=jnp.float32)
        if last:
            mixed[i, at : at + tile] = (earlier[i, at : at + tile] + acc).astype(jnp.bfloat16)
        else:
            mixed[i, at : at + tile] = acc
    gwt = jnp.dot(cott[...], basis[...], preferred_element_type=jnp.float32)
    dhalf = chan // 2
    at = nk if last else 0
    if last:
        keep[0:nk] = keep_in[...]
        send[0:nk] = send_in[...]
    for k in range(nk):
        mat = gwt[:, k * HALF : (k + 1) * HALF].T
        low, high = mat[:, :dhalf], mat[:, dhalf:]
        keep[at + k] = jnp.where(odd, high, low)
        send[at + k] = jnp.where(odd, low, high).astype(jnp.bfloat16)


def forward(table, own, near, far, fast, cot, weight, h, earlier=()):
    rows, width, chan = cot.shape
    nk = weight.shape[0]
    smem = pl.BlockSpec(memory_space=pltpu.SMEM)
    vmem = pl.BlockSpec(memory_space=pltpu.VMEM)
    last = len(earlier) > 0
    count = nk * (1 + last)
    half = pl.BlockSpec((rows, width, HALF), lambda g: (0, 0, h))
    side = pl.BlockSpec((H, width, HALF), lambda g: (0, 0, h))
    wide = pl.BlockSpec((rows, width, chan), lambda g: (0, 0, 0))
    edge = pl.BlockSpec((H, width, HALF), lambda g: (0, 0, 0))

    def part(blocks):
        return pl.BlockSpec((blocks, HALF, chan // 2), lambda g: (0, 0, 0))

    return pl.pallas_call(
        lambda *refs: fwd_kernel(last, *refs),
        grid=(1,),
        in_specs=[smem]
        + [half, edge, side, side, wide, pl.BlockSpec((nk, HALF, chan), lambda g: (0, h, 0))]
        + ([wide, part(nk), part(nk)] if last else []),
        out_specs=[wide, part(count), part(count)],
        out_shape=[
            jax.ShapeDtypeStruct((rows, width, chan), jnp.bfloat16 if last else jnp.float32),
            jax.ShapeDtypeStruct((count, HALF, chan // 2), jnp.float32),
            jax.ShapeDtypeStruct((count, HALF, chan // 2), jnp.bfloat16),
        ],
        scratch_shapes=[
            pltpu.VMEM((rows + 2 * H, width + 2 * PAD, HALF), jnp.float32),
            pltpu.VMEM((rows * width, nk * HALF), jnp.bfloat16),
            pltpu.VMEM((chan, rows * width), jnp.bfloat16),
        ],
        compiler_params=pltpu.CompilerParams(vmem_limit_bytes=32 * 2**20),
        cost_estimate=pl.CostEstimate(
            flops=0, bytes_accessed=0, transcendentals=0
        ),
        name="forward",
    )(table, own, near, far, fast, cot, weight, *earlier)


def bwd_kernel(table, cin, win, own, *rest):
    edges, scratch = rest[:2], rest[2:]
    db, acc, narrow, cnt, lst_n, lst_o, lst_v, out_sems = scratch
    rows, width, chan = cin.shape
    nk = win.shape[0]
    ne = table.shape[2] // 3
    odd = table[0, 0, 3 * ne] > 0.5
    nh = chan // HALF
    lines = rows + 2 * H
    cap = rows * nk * ne + 2 * GROUP
    for line in range(lines):
        cnt[line] = 0

    for i in range(rows):

        def bin_one(k, carry):
            for e in range(ne):
                row, lon, value = entry(table, i, k, e, ne)
                line = i + H + row
                c = cnt[line]
                lst_n[line * cap + c] = i * nk + k
                lst_o[line * cap + c] = PAD - lon
                lst_v[line * cap + c] = value
                cnt[line] = c + 1
            return carry

        for k in range(nk):
            bin_one(k, 0)
    for line in range(lines):
        c = cnt[line]
        for g in range(2 * GROUP):
            lst_n[line * cap + c + g] = 0
            lst_o[line * cap + c + g] = PAD
            lst_v[line * cap + c + g] = 0.0
    for i in range(rows):
        for k in range(nk):
            n = i * nk + k
            d = lax.dot_general(
                cin[i], win[k], (((1,), (1,)), ((), ())), preferred_element_type=jnp.float32
            )
            for h in range(nh):
                cols = slice(h * HALF, (h + 1) * HALF)
                db[n, h, PAD : PAD + width] = d[:, cols]
                db[n, h, 0:PAD] = d[width - PAD :, cols]
                db[n, h, PAD + width :] = d[0:PAD, cols]

    def terms(t, g, h):
        s = None
        for j in range(GROUP):
            at = t * cap + g * GROUP + j
            x = lst_v[at] * db[lst_n[at], h, pl.ds(lst_o[at], width), :]
            s = x if s is None else s + x
        return s

    def line_sum(t, slot, dst, row):
        groups = jnp.maximum((cnt[t] + GROUP - 1) // GROUP, 2)
        for h in range(nh):
            acc[slot, :, h * HALF : (h + 1) * HALF] = terms(t, 0, h)

        def group(g, carry):
            for h in range(nh):
                cols = slice(h * HALF, (h + 1) * HALF)
                acc[slot, :, cols] = acc[slot, :, cols] + terms(t, g, h)
            return carry

        lax.fori_loop(1, groups - 1, group, 0)
        for h in range(nh):
            cols = slice(h * HALF, (h + 1) * HALF)
            total = acc[slot, :, cols] + terms(t, groups - 1, h)
            dst[row, :, cols] = total.astype(dst.dtype)

    def edge(s, carry):
        top = (s < H) != odd
        line_sum(jnp.where(top, 0, H + rows) + s % H, rows, narrow, s)
        return carry

    lax.fori_loop(0, 2 * H, edge, 0)
    writes = [
        pltpu.make_async_copy(narrow.at[0:H], edges[0], out_sems.at[0]),
        pltpu.make_async_copy(narrow.at[H:], edges[1], out_sems.at[1]),
    ]
    for r in range(rows):
        writes.append(pltpu.make_async_copy(acc.at[r], own.at[r], out_sems.at[2 + r]))
    for write in writes[:2]:
        write.start()
    for r in range(rows):
        line_sum(H + r, r, acc, r)
        writes[2 + r].start()
    for write in writes:
        write.wait()


def backward(table, cot, weight):
    rows, width, chan = cot.shape
    nk = weight.shape[0]
    ne = table.shape[2] // 3
    smem = pl.BlockSpec(memory_space=pltpu.SMEM)
    anym = pl.BlockSpec(memory_space=pl.ANY)
    lines = rows + 2 * H
    cap = rows * nk * ne + 2 * GROUP
    return pl.pallas_call(
        bwd_kernel,
        in_specs=[smem] + [pl.BlockSpec(memory_space=pltpu.VMEM)] * 2,
        out_specs=[anym] * 3,
        out_shape=[
            jax.ShapeDtypeStruct((rows, width, chan), jnp.float32),
        ]
        + [jax.ShapeDtypeStruct((H, width, chan), jnp.bfloat16)] * 2,
        scratch_shapes=[
            pltpu.VMEM((rows * nk, chan // HALF, width + 2 * PAD, HALF), jnp.float32),
            pltpu.VMEM((rows + 1, width, chan), jnp.float32),
            pltpu.VMEM((2 * H, width, chan), jnp.bfloat16),
            pltpu.SMEM((lines,), jnp.int32),
            pltpu.SMEM((lines * cap,), jnp.int32),
            pltpu.SMEM((lines * cap,), jnp.int32),
            pltpu.SMEM((lines * cap,), jnp.float32),
            pltpu.SemaphoreType.DMA((2 + rows,)),
        ],
        compiler_params=pltpu.CompilerParams(vmem_limit_bytes=56 * 2**20),
        cost_estimate=pl.CostEstimate(flops=0, bytes_accessed=0, transcendentals=0),
        name="backward",
    )(table, cot, weight)


WAITS = (-1, 3)
ADDED = 4
TIED = True


def swap(value, bit, size):
    return lax.ppermute(value, "lat", [(i, i ^ bit) for i in range(size)])


def sum_over_lat(keep, send, between):
    size = lax.axis_size("lat")
    shape = keep.shape
    index = lax.axis_index("lat")
    whole = keep.reshape(-1, shape[-1])
    whole = whole + swap(send.reshape(-1, shape[-1]), 1, size).astype(jnp.float32)
    (whole,) = between(-1, [whole])
    values = list(jnp.split(whole, 2))
    rest = [1 << b for b in range(1, size.bit_length() - 1)]
    orders = [rest[1:] + rest[:1], rest]
    for step in range(len(rest) - 1):
        values = between(step, values)
        for j in range(2):
            bit = orders[j][step]
            side = (index // bit) % 2
            count = values[j].shape[0] // 2
            kept = lax.dynamic_slice_in_dim(values[j], side * count, count, 0)
            sent = lax.dynamic_slice_in_dim(values[j], (1 - side) * count, count, 0)
            got = swap(sent.astype(jnp.bfloat16), bit, size)
            values[j] = kept + got.astype(jnp.float32)
    values = between(len(rest) - 1, values)
    for j in range(2):
        sent = values[j].astype(jnp.bfloat16)
        got = swap(sent, orders[j][-1], size)
        values[j] = (sent.astype(jnp.float32) + got.astype(jnp.float32)).astype(jnp.bfloat16)
    for step in reversed(range(len(rest) - 1)):
        values = between(2 * len(rest) - 2 - step, values)
        for j in range(2):
            bit = orders[j][step]
            side = (index // bit) % 2
            got = swap(values[j], bit, size)
            values[j] = jnp.where(
                side == 0,
                jnp.concatenate([values[j], got]),
                jnp.concatenate([got, values[j]]),
            )
    values = between(2 * len(rest) - 1, values)
    parts = []
    for value in values:
        got = swap(value, 1, size)
        first = jnp.where(index % 2 == 0, value, got)
        second = jnp.where(index % 2 == 0, got, value)
        part = (shape[0] // 2, *shape[1:])
        parts.append(jnp.concatenate([first.reshape(part), second.reshape(part)], axis=-1))
    return jnp.concatenate(parts, axis=1)


def per_device(inputs, cotangent, weight, pat_rows, pat_lons, pat_vals):
    rows = inputs.shape[0]
    width = inputs.shape[1]
    size = lax.axis_size("lat")
    index = lax.axis_index("lat")
    odd = index % 2 == 1
    fast_pairs = [(i, i ^ 1) for i in range(size)]
    slow_pairs = [(i, i + 1 if i % 2 else i - 1) for i in range(1, size - 1)]
    near_pairs = [pair for pair in slow_pairs if min(pair) % 4 == 1]
    far_pairs = [pair for pair in slow_pairs if min(pair) % 4 == 3]
    if rows == H:
        to_slow = to_fast = inputs
    else:
        head, tail = inputs[:H], inputs[rows - H :]
        to_slow, to_fast = jnp.where(odd, tail, head), jnp.where(odd, head, tail)
    far = lax.ppermute(to_slow, "lat", far_pairs)
    part = to_slow[:, :, :HALF]
    near = [lax.ppermute(part, "lat", near_pairs)]
    rest, part = lax.optimization_barrier((to_slow, part))
    near.append(lax.ppermute(rest[:, :, HALF:], "lat", near_pairs))
    fast = lax.ppermute(to_fast, "lat", fast_pairs)
    side = jnp.full((rows, pat_rows.shape[1], 1), odd, jnp.float32)
    table = [
        lax.dynamic_slice_in_dim(part, index * rows, rows, 0).astype(jnp.float32)
        for part in (pat_rows, pat_lons, pat_vals)
    ]
    table = jnp.concatenate([*table, side], axis=-1)
    grad, edge_slow, edge_fast = backward(table, cotangent, weight)
    near[0], far, fast, edge_slow, edge_fast = lax.optimization_barrier(
        (near[0], far, fast, edge_slow, edge_fast)
    )
    partial, *earlier = forward(table, inputs, near[0], far, fast, cotangent, weight, 0)
    partial, edge_slow, edge_fast = lax.optimization_barrier((partial, edge_slow, edge_fast))
    got_far = lax.ppermute(edge_slow, "lat", far_pairs)
    got_near = lax.ppermute(edge_slow, "lat", near_pairs)
    got_fast = lax.ppermute(edge_fast, "lat", fast_pairs)
    mixed, keep, send = forward(table, inputs, near[1], far, fast, cotangent, weight, 1, (partial, *earlier))
    scale = 1.0 / math.sqrt(pat_rows.shape[0] * width)
    got = [got_far, got_near, got_fast]

    def between(step, values):
        nonlocal grad
        for j in range(2):
            if step == WAITS[j]:
                values, got[j] = lax.optimization_barrier((values, got[j]))
        if step == WAITS[0]:
            values, got[2] = lax.optimization_barrier((values, got[2]))
        if step == ADDED:
            from_slow = got[0].astype(jnp.float32) + got[1].astype(jnp.float32)
            from_fast = got[2].astype(jnp.float32)
            if rows == H:
                grad = grad + from_slow + from_fast
            else:
                grad = grad.at[:H].add(jnp.where(odd, from_fast, from_slow))
                grad = grad.at[rows - H :].add(jnp.where(odd, from_slow, from_fast))
            grad = grad.astype(jnp.bfloat16)
            if TIED:
                values, grad = lax.optimization_barrier((values, grad))
        return list(values)

    total = sum_over_lat(keep, send, between)
    return (mixed, grad, total.astype(jnp.float32) * scale)


def solution(mesh):
    return jax.shard_map(
        per_device,
        mesh=mesh,
        in_specs=(
            P(("group", "lat"), None, None),
            P(("group", "lat"), None, None),
            P(),
            P(),
            P(),
            P(),
        ),
        out_specs=(
            P(("group", "lat"), None, None),
            P(("group", "lat"), None, None),
            P("group", None, None),
        ),
        check_vma=False,
    )
```

```python
import math

import jax
import jax.numpy as jnp
from jax import lax
from jax.experimental import pallas as pl
from jax.experimental.pallas import tpu as pltpu
from jax.sharding import PartitionSpec as P

H = 2
PAD = 16
GROUP = 4
HALF = 128


def entry(table, i, k, e, ne):
    return (
        table[i, k, e].astype(jnp.int32),
        table[i, k, ne + e].astype(jnp.int32),
        table[i, k, 2 * ne + e],
    )


def fwd_kernel(last, table, *refs):
    if last:
        own, near, far, fast, cot, weight, earlier, keep_in, send_in, mixed, keep, send, xf, basis, cott = refs
    else:
        own, near, far, fast, cot, weight, mixed, keep, send, xf, basis, cott = refs
    rows, width, _ = own.shape
    chan = cot.shape[2]
    nk = weight.shape[0]
    ne = table.shape[2] // 3
    odd = table[0, 0, 3 * ne] > 0.5

    def widen(src, r, dst, more=None):
        def part(at, to):
            piece = src[r, at].astype(jnp.float32)
            if more is not None:
                piece = piece + more[r, at].astype(jnp.float32)
            xf[dst, to] = piece

        part(slice(0, width), slice(PAD, PAD + width))
        part(slice(width - PAD, width), slice(0, PAD))
        part(slice(0, PAD), slice(PAD + width, 2 * PAD + width))

    for r in range(H):
        widen(near, r, jnp.where(odd, H + rows, 0) + r, far)
        widen(fast, r, jnp.where(odd, 0, H + rows) + r)
    for r in range(rows):
        widen(own, r, H + r)
        cott[:, r * width : (r + 1) * width] = cot[r].T
    for i in range(rows):

        def per_k(k, carry):
            t = None
            for e in range(ne):
                line, lon, value = entry(table, i, k, e, ne)
                term = value * xf[i + H + line, pl.ds(PAD + lon, width), :]
                t = term if t is None else t + term
            cols = pl.ds(pl.multiple_of(k * HALF, HALF), HALF)
            basis[i * width : (i + 1) * width, cols] = t.astype(jnp.bfloat16)
            return carry

        lax.fori_loop(0, nk, per_k, 0)
    wflat = weight[...].reshape(nk * HALF, chan)
    parts = 3 * rows
    tile = rows * width // parts
    for p in range(parts):
        i, at = divmod(p * tile, width)
        acc = jnp.dot(basis[p * tile : (p + 1) * tile], wflat, preferred_element_type=jnp.float32)
        if last:
            mixed[i, at : at + tile] = (earlier[i, at : at + tile] + acc).astype(jnp.bfloat16)
        else:
            mixed[i, at : at + tile] = acc
    gwt = jnp.dot(cott[...], basis[...], preferred_element_type=jnp.float32)
    dhalf = chan // 2
    at = nk if last else 0
    if last:
        keep[0:nk] = keep_in[...]
        send[0:nk] = send_in[...]
    for k in range(nk):
        mat = gwt[:, k * HALF : (k + 1) * HALF].T
        low, high = mat[:, :dhalf], mat[:, dhalf:]
        keep[at + k] = jnp.where(odd, high, low)
        send[at + k] = jnp.where(odd, low, high).astype(jnp.bfloat16)


def forward(table, own, near, far, fast, cot, weight, h, earlier=()):
    rows, width, chan = cot.shape
    nk = weight.shape[0]
    smem = pl.BlockSpec(memory_space=pltpu.SMEM)
    vmem = pl.BlockSpec(memory_space=pltpu.VMEM)
    last = len(earlier) > 0
    count = nk * (1 + last)
    half = pl.BlockSpec((rows, width, HALF), lambda g: (0, 0, h))
    side = pl.BlockSpec((H, width, HALF), lambda g: (0, 0, h))
    wide = pl.BlockSpec((rows, width, chan), lambda g: (0, 0, 0))
    edge = pl.BlockSpec((H, width, HALF), lambda g: (0, 0, 0))

    def part(blocks):
        return pl.BlockSpec((blocks, HALF, chan // 2), lambda g: (0, 0, 0))

    return pl.pallas_call(
        lambda *refs: fwd_kernel(last, *refs),
        grid=(1,),
        in_specs=[smem]
        + [half, edge, side, side, wide, pl.BlockSpec((nk, HALF, chan), lambda g: (0, h, 0))]
        + ([wide, part(nk), part(nk)] if last else []),
        out_specs=[wide, part(count), part(count)],
        out_shape=[
            jax.ShapeDtypeStruct((rows, width, chan), jnp.bfloat16 if last else jnp.float32),
            jax.ShapeDtypeStruct((count, HALF, chan // 2), jnp.float32),
            jax.ShapeDtypeStruct((count, HALF, chan // 2), jnp.bfloat16),
        ],
        scratch_shapes=[
            pltpu.VMEM((rows + 2 * H, width + 2 * PAD, HALF), jnp.float32),
            pltpu.VMEM((rows * width, nk * HALF), jnp.bfloat16),
            pltpu.VMEM((chan, rows * width), jnp.bfloat16),
        ],
        compiler_params=pltpu.CompilerParams(vmem_limit_bytes=32 * 2**20),
        cost_estimate=pl.CostEstimate(
            flops=0, bytes_accessed=0, transcendentals=0
        ),
        name="forward",
    )(table, own, near, far, fast, cot, weight, *earlier)


def bwd_kernel(table, cin, win, own, *rest):
    edges, scratch = rest[:2], rest[2:]
    db, acc, narrow, cnt, lst_n, lst_o, lst_v, out_sems = scratch
    rows, width, chan = cin.shape
    nk = win.shape[0]
    ne = table.shape[2] // 3
    odd = table[0, 0, 3 * ne] > 0.5
    nh = chan // HALF
    lines = rows + 2 * H
    cap = rows * nk * ne + 2 * GROUP
    for line in range(lines):
        cnt[line] = 0

    for i in range(rows):

        def bin_one(k, carry):
            for e in range(ne):
                row, lon, value = entry(table, i, k, e, ne)
                line = i + H + row
                c = cnt[line]
                lst_n[line * cap + c] = i * nk + k
                lst_o[line * cap + c] = PAD - lon
                lst_v[line * cap + c] = value
                cnt[line] = c + 1
            return carry

        for k in range(nk):
            bin_one(k, 0)
    for line in range(lines):
        c = cnt[line]
        for g in range(2 * GROUP):
            lst_n[line * cap + c + g] = 0
            lst_o[line * cap + c + g] = PAD
            lst_v[line * cap + c + g] = 0.0
    for i in range(rows):
        for k in range(nk):
            n = i * nk + k
            d = lax.dot_general(
                cin[i], win[k], (((1,), (1,)), ((), ())), preferred_element_type=jnp.float32
            )
            for h in range(nh):
                cols = slice(h * HALF, (h + 1) * HALF)
                db[n, h, PAD : PAD + width] = d[:, cols]
                db[n, h, 0:PAD] = d[width - PAD :, cols]
                db[n, h, PAD + width :] = d[0:PAD, cols]

    def terms(t, g, h):
        s = None
        for j in range(GROUP):
            at = t * cap + g * GROUP + j
            x = lst_v[at] * db[lst_n[at], h, pl.ds(lst_o[at], width), :]
            s = x if s is None else s + x
        return s

    def line_sum(t, slot, dst, row):
        groups = jnp.maximum((cnt[t] + GROUP - 1) // GROUP, 2)
        for h in range(nh):
            acc[slot, :, h * HALF : (h + 1) * HALF] = terms(t, 0, h)

        def group(g, carry):
            for h in range(nh):
                cols = slice(h * HALF, (h + 1) * HALF)
                acc[slot, :, cols] = acc[slot, :, cols] + terms(t, g, h)
            return carry

        lax.fori_loop(1, groups - 1, group, 0)
        for h in range(nh):
            cols = slice(h * HALF, (h + 1) * HALF)
            total = acc[slot, :, cols] + terms(t, groups - 1, h)
            dst[row, :, cols] = total.astype(dst.dtype)

    def edge(s, carry):
        top = (s < H) != odd
        line_sum(jnp.where(top, 0, H + rows) + s % H, rows, narrow, s)
        return carry

    lax.fori_loop(0, 2 * H, edge, 0)
    writes = [
        pltpu.make_async_copy(narrow.at[0:H], edges[0], out_sems.at[0]),
        pltpu.make_async_copy(narrow.at[H:], edges[1], out_sems.at[1]),
    ]
    for r in range(rows):
        writes.append(pltpu.make_async_copy(acc.at[r], own.at[r], out_sems.at[2 + r]))
    for write in writes[:2]:
        write.start()
    for r in range(rows):
        line_sum(H + r, r, acc, r)
        writes[2 + r].start()
    for write in writes:
        write.wait()


def backward(table, cot, weight):
    rows, width, chan = cot.shape
    nk = weight.shape[0]
    ne = table.shape[2] // 3
    smem = pl.BlockSpec(memory_space=pltpu.SMEM)
    anym = pl.BlockSpec(memory_space=pl.ANY)
    lines = rows + 2 * H
    cap = rows * nk * ne + 2 * GROUP
    return pl.pallas_call(
        bwd_kernel,
        in_specs=[smem] + [pl.BlockSpec(memory_space=pltpu.VMEM)] * 2,
        out_specs=[anym] * 3,
        out_shape=[
            jax.ShapeDtypeStruct((rows, width, chan), jnp.float32),
        ]
        + [jax.ShapeDtypeStruct((H, width, chan), jnp.bfloat16)] * 2,
        scratch_shapes=[
            pltpu.VMEM((rows * nk, chan // HALF, width + 2 * PAD, HALF), jnp.float32),
            pltpu.VMEM((rows + 1, width, chan), jnp.float32),
            pltpu.VMEM((2 * H, width, chan), jnp.bfloat16),
            pltpu.SMEM((lines,), jnp.int32),
            pltpu.SMEM((lines * cap,), jnp.int32),
            pltpu.SMEM((lines * cap,), jnp.int32),
            pltpu.SMEM((lines * cap,), jnp.float32),
            pltpu.SemaphoreType.DMA((2 + rows,)),
        ],
        compiler_params=pltpu.CompilerParams(vmem_limit_bytes=56 * 2**20),
        cost_estimate=pl.CostEstimate(flops=0, bytes_accessed=0, transcendentals=0),
        name="backward",
    )(table, cot, weight)


WAITS = (-1, 3)
ADDED = 4
TIED = True


def swap(value, bit, size):
    return lax.ppermute(value, "lat", [(i, i ^ bit) for i in range(size)])


def sum_over_lat(keep, send, between):
    size = lax.axis_size("lat")
    shape = keep.shape
    index = lax.axis_index("lat")
    whole = keep.reshape(-1, shape[-1])
    whole = whole + swap(send.reshape(-1, shape[-1]), 1, size).astype(jnp.float32)
    (whole,) = between(-1, [whole])
    values = list(jnp.split(whole, 2))
    rest = [1 << b for b in range(1, size.bit_length() - 1)]
    orders = [rest[1:] + rest[:1], rest]
    for step in range(len(rest) - 1):
        values = between(step, values)
        for j in range(2):
            bit = orders[j][step]
            side = (index // bit) % 2
            count = values[j].shape[0] // 2
            kept = lax.dynamic_slice_in_dim(values[j], side * count, count, 0)
            sent = lax.dynamic_slice_in_dim(values[j], (1 - side) * count, count, 0)
            got = swap(sent.astype(jnp.bfloat16), bit, size)
            values[j] = kept + got.astype(jnp.float32)
    values = between(len(rest) - 1, values)
    for j in range(2):
        sent = values[j].astype(jnp.bfloat16)
        got = swap(sent, orders[j][-1], size)
        values[j] = (sent.astype(jnp.float32) + got.astype(jnp.float32)).astype(jnp.bfloat16)
    for step in reversed(range(len(rest) - 1)):
        values = between(2 * len(rest) - 2 - step, values)
        for j in range(2):
            bit = orders[j][step]
            side = (index // bit) % 2
            got = swap(values[j], bit, size)
            values[j] = jnp.where(
                side == 0,
                jnp.concatenate([values[j], got]),
                jnp.concatenate([got, values[j]]),
            )
    values = between(2 * len(rest) - 1, values)
    parts = []
    for value in values:
        got = swap(value, 1, size)
        first = jnp.where(index % 2 == 0, value, got)
        second = jnp.where(index % 2 == 0, got, value)
        part = (shape[0] // 2, *shape[1:])
        parts.append(jnp.concatenate([first.reshape(part), second.reshape(part)], axis=-1))
    return jnp.concatenate(parts, axis=1)


def per_device(inputs, cotangent, weight, pat_rows, pat_lons, pat_vals):
    rows = inputs.shape[0]
    width = inputs.shape[1]
    size = lax.axis_size("lat")
    index = lax.axis_index("lat")
    odd = index % 2 == 1
    fast_pairs = [(i, i ^ 1) for i in range(size)]
    slow_pairs = [(i, i + 1 if i % 2 else i - 1) for i in range(1, size - 1)]
    near_pairs = [pair for pair in slow_pairs if min(pair) % 4 == 1]
    far_pairs = [pair for pair in slow_pairs if min(pair) % 4 == 3]
    if rows == H:
        to_slow = to_fast = inputs
    else:
        head, tail = inputs[:H], inputs[rows - H :]
        to_slow, to_fast = jnp.where(odd, tail, head), jnp.where(odd, head, tail)
    far = lax.ppermute(to_slow, "lat", far_pairs)
    part = to_slow[:, :, :HALF]
    near = [lax.ppermute(part, "lat", near_pairs)]
    rest, part = lax.optimization_barrier((to_slow, part))
    near.append(lax.ppermute(rest[:, :, HALF:], "lat", near_pairs))
    fast = lax.ppermute(to_fast, "lat", fast_pairs)
    side = jnp.full((rows, pat_rows.shape[1], 1), odd, jnp.float32)
    table = [
        lax.dynamic_slice_in_dim(part, index * rows, rows, 0).astype(jnp.float32)
        for part in (pat_rows, pat_lons, pat_vals)
    ]
    table = jnp.concatenate([*table, side], axis=-1)
    grad, edge_slow, edge_fast = backward(table, cotangent, weight)
    near[0], far, fast, edge_slow, edge_fast = lax.optimization_barrier(
        (near[0], far, fast, edge_slow, edge_fast)
    )
    partial, *earlier = forward(table, inputs, near[0], far, fast, cotangent, weight, 0)
    partial, edge_slow, edge_fast = lax.optimization_barrier((partial, edge_slow, edge_fast))
    got_far = lax.ppermute(edge_slow, "lat", far_pairs)
    got_near = lax.ppermute(edge_slow, "lat", near_pairs)
    got_fast = lax.ppermute(edge_fast, "lat", fast_pairs)
    mixed, keep, send = forward(table, inputs, near[1], far, fast, cotangent, weight, 1, (partial, *earlier))
    scale = 1.0 / math.sqrt(pat_rows.shape[0] * width)
    got = [got_far, got_near, got_fast]

    def between(step, values):
        nonlocal grad
        for j in range(2):
            if step == WAITS[j] and j == 0:
                values, got[j] = lax.optimization_barrier((values, got[j]))
            elif step == WAITS[j]:
                values = list(values)
                values[1], got[j] = lax.optimization_barrier((values[1], got[j]))
        if step == WAITS[0]:
            values, got[2] = lax.optimization_barrier((values, got[2]))
        if step == ADDED:
            from_slow = got[0].astype(jnp.float32) + got[1].astype(jnp.float32)
            from_fast = got[2].astype(jnp.float32)
            if rows == H:
                grad = grad + from_slow + from_fast
            else:
                grad = grad.at[:H].add(jnp.where(odd, from_fast, from_slow))
                grad = grad.at[rows - H :].add(jnp.where(odd, from_slow, from_fast))
            grad = grad.astype(jnp.bfloat16)
            if TIED:
                values, grad = lax.optimization_barrier((values, grad))
        return list(values)

    total = sum_over_lat(keep, send, between)
    return (mixed, grad, total.astype(jnp.float32) * scale)


def solution(mesh):
    return jax.shard_map(
        per_device,
        mesh=mesh,
        in_specs=(
            P(("group", "lat"), None, None),
            P(("group", "lat"), None, None),
            P(),
            P(),
            P(),
            P(),
        ),
        out_specs=(
            P(("group", "lat"), None, None),
            P(("group", "lat"), None, None),
            P("group", None, None),
        ),
        check_vma=False,
    )
```

```python
import math

import jax
import jax.numpy as jnp
from jax import lax
from jax.experimental import pallas as pl
from jax.experimental.pallas import tpu as pltpu
from jax.sharding import PartitionSpec as P

H = 2
PAD = 16
GROUP = 4
HALF = 128


def entry(table, i, k, e, ne):
    return (
        table[i, k, e].astype(jnp.int32),
        table[i, k, ne + e].astype(jnp.int32),
        table[i, k, 2 * ne + e],
    )


def fwd_kernel(last, table, *refs):
    if last:
        own, near, far, fast, cot, weight, earlier, keep_in, send_in, mixed, keep, send, xf, basis, cott = refs
    else:
        own, near, far, fast, cot, weight, mixed, keep, send, xf, basis, cott = refs
    rows, width, _ = own.shape
    chan = cot.shape[2]
    nk = weight.shape[0]
    ne = table.shape[2] // 3
    odd = table[0, 0, 3 * ne] > 0.5

    def widen(src, r, dst, more=None):
        def part(at, to):
            piece = src[r, at].astype(jnp.float32)
            if more is not None:
                piece = piece + more[r, at].astype(jnp.float32)
            xf[dst, to] = piece

        part(slice(0, width), slice(PAD, PAD + width))
        part(slice(width - PAD, width), slice(0, PAD))
        part(slice(0, PAD), slice(PAD + width, 2 * PAD + width))

    for r in range(H):
        widen(near, r, jnp.where(odd, H + rows, 0) + r, far)
        widen(fast, r, jnp.where(odd, 0, H + rows) + r)
    for r in range(rows):
        widen(own, r, H + r)
        cott[:, r * width : (r + 1) * width] = cot[r].T
    for i in range(rows):

        def per_k(k, carry):
            t = None
            for e in range(ne):
                line, lon, value = entry(table, i, k, e, ne)
                term = value * xf[i + H + line, pl.ds(PAD + lon, width), :]
                t = term if t is None else t + term
            cols = pl.ds(pl.multiple_of(k * HALF, HALF), HALF)
            basis[i * width : (i + 1) * width, cols] = t.astype(jnp.bfloat16)
            return carry

        lax.fori_loop(0, nk, per_k, 0, unroll=3)
    wflat = weight[...].reshape(nk * HALF, chan)
    parts = 3 * rows
    tile = rows * width // parts
    for p in range(parts):
        i, at = divmod(p * tile, width)
        acc = jnp.dot(basis[p * tile : (p + 1) * tile], wflat, preferred_element_type=jnp.float32)
        if last:
            mixed[i, at : at + tile] = (earlier[i, at : at + tile] + acc).astype(jnp.bfloat16)
        else:
            mixed[i, at : at + tile] = acc
    gwt = jnp.dot(cott[...], basis[...], preferred_element_type=jnp.float32)
    dhalf = chan // 2
    at = nk if last else 0
    if last:
        keep[0:nk] = keep_in[...]
        send[0:nk] = send_in[...]
    for k in range(nk):
        mat = gwt[:, k * HALF : (k + 1) * HALF].T
        low, high = mat[:, :dhalf], mat[:, dhalf:]
        keep[at + k] = jnp.where(odd, high, low)
        send[at + k] = jnp.where(odd, low, high).astype(jnp.bfloat16)


def forward(table, own, near, far, fast, cot, weight, h, earlier=()):
    rows, width, chan = cot.shape
    nk = weight.shape[0]
    smem = pl.BlockSpec(memory_space=pltpu.SMEM)
    vmem = pl.BlockSpec(memory_space=pltpu.VMEM)
    last = len(earlier) > 0
    count = nk * (1 + last)
    half = pl.BlockSpec((rows, width, HALF), lambda g: (0, 0, h))
    side = pl.BlockSpec((H, width, HALF), lambda g: (0, 0, h))
    wide = pl.BlockSpec((rows, width, chan), lambda g: (0, 0, 0))
    edge = pl.BlockSpec((H, width, HALF), lambda g: (0, 0, 0))

    def part(blocks):
        return pl.BlockSpec((blocks, HALF, chan // 2), lambda g: (0, 0, 0))

    return pl.pallas_call(
        lambda *refs: fwd_kernel(last, *refs),
        grid=(1,),
        in_specs=[smem]
        + [half, edge, side, side, wide, pl.BlockSpec((nk, HALF, chan), lambda g: (0, h, 0))]
        + ([wide, part(nk), part(nk)] if last else []),
        out_specs=[wide, part(count), part(count)],
        out_shape=[
            jax.ShapeDtypeStruct((rows, width, chan), jnp.bfloat16 if last else jnp.float32),
            jax.ShapeDtypeStruct((count, HALF, chan // 2), jnp.float32),
            jax.ShapeDtypeStruct((count, HALF, chan // 2), jnp.bfloat16),
        ],
        scratch_shapes=[
            pltpu.VMEM((rows + 2 * H, width + 2 * PAD, HALF), jnp.float32),
            pltpu.VMEM((rows * width, nk * HALF), jnp.bfloat16),
            pltpu.VMEM((chan, rows * width), jnp.bfloat16),
        ],
        compiler_params=pltpu.CompilerParams(vmem_limit_bytes=32 * 2**20),
        cost_estimate=pl.CostEstimate(
            flops=0, bytes_accessed=0, transcendentals=0
        ),
        name="forward",
    )(table, own, near, far, fast, cot, weight, *earlier)


def bwd_kernel(table, cin, win, own, *rest):
    edges, scratch = rest[:2], rest[2:]
    db, acc, narrow, cnt, lst_n, lst_o, lst_v, out_sems = scratch
    rows, width, chan = cin.shape
    nk = win.shape[0]
    ne = table.shape[2] // 3
    odd = table[0, 0, 3 * ne] > 0.5
    nh = chan // HALF
    lines = rows + 2 * H
    cap = rows * nk * ne + 2 * GROUP
    for line in range(lines):
        cnt[line] = 0

    for i in range(rows):

        def bin_one(k, carry):
            for e in range(ne):
                row, lon, value = entry(table, i, k, e, ne)
                line = i + H + row
                c = cnt[line]
                lst_n[line * cap + c] = i * nk + k
                lst_o[line * cap + c] = PAD - lon
                lst_v[line * cap + c] = value
                cnt[line] = c + 1
            return carry

        for k in range(nk):
            bin_one(k, 0)
    for line in range(lines):
        c = cnt[line]
        for g in range(2 * GROUP):
            lst_n[line * cap + c + g] = 0
            lst_o[line * cap + c + g] = PAD
            lst_v[line * cap + c + g] = 0.0
    for i in range(rows):
        for k in range(nk):
            n = i * nk + k
            d = lax.dot_general(
                cin[i], win[k], (((1,), (1,)), ((), ())), preferred_element_type=jnp.float32
            )
            for h in range(nh):
                cols = slice(h * HALF, (h + 1) * HALF)
                db[n, h, PAD : PAD + width] = d[:, cols]
                db[n, h, 0:PAD] = d[width - PAD :, cols]
                db[n, h, PAD + width :] = d[0:PAD, cols]

    def terms(t, g, h):
        s = None
        for j in range(GROUP):
            at = t * cap + g * GROUP + j
            x = lst_v[at] * db[lst_n[at], h, pl.ds(lst_o[at], width), :]
            s = x if s is None else s + x
        return s

    def line_sum(t, slot, dst, row):
        groups = jnp.maximum((cnt[t] + GROUP - 1) // GROUP, 2)
        for h in range(nh):
            acc[slot, :, h * HALF : (h + 1) * HALF] = terms(t, 0, h)

        def group(g, carry):
            for h in range(nh):
                cols = slice(h * HALF, (h + 1) * HALF)
                acc[slot, :, cols] = acc[slot, :, cols] + terms(t, g, h)
            return carry

        lax.fori_loop(1, groups - 1, group, 0)
        for h in range(nh):
            cols = slice(h * HALF, (h + 1) * HALF)
            total = acc[slot, :, cols] + terms(t, groups - 1, h)
            dst[row, :, cols] = total.astype(dst.dtype)

    def edge(s, carry):
        top = (s < H) != odd
        line_sum(jnp.where(top, 0, H + rows) + s % H, rows, narrow, s)
        return carry

    lax.fori_loop(0, 2 * H, edge, 0)
    writes = [
        pltpu.make_async_copy(narrow.at[0:H], edges[0], out_sems.at[0]),
        pltpu.make_async_copy(narrow.at[H:], edges[1], out_sems.at[1]),
    ]
    for r in range(rows):
        writes.append(pltpu.make_async_copy(acc.at[r], own.at[r], out_sems.at[2 + r]))
    for write in writes[:2]:
        write.start()
    for r in range(rows):
        line_sum(H + r, r, acc, r)
        writes[2 + r].start()
    for write in writes:
        write.wait()


def backward(table, cot, weight):
    rows, width, chan = cot.shape
    nk = weight.shape[0]
    ne = table.shape[2] // 3
    smem = pl.BlockSpec(memory_space=pltpu.SMEM)
    anym = pl.BlockSpec(memory_space=pl.ANY)
    lines = rows + 2 * H
    cap = rows * nk * ne + 2 * GROUP
    return pl.pallas_call(
        bwd_kernel,
        in_specs=[smem] + [pl.BlockSpec(memory_space=pltpu.VMEM)] * 2,
        out_specs=[anym] * 3,
        out_shape=[
            jax.ShapeDtypeStruct((rows, width, chan), jnp.float32),
        ]
        + [jax.ShapeDtypeStruct((H, width, chan), jnp.bfloat16)] * 2,
        scratch_shapes=[
            pltpu.VMEM((rows * nk, chan // HALF, width + 2 * PAD, HALF), jnp.float32),
            pltpu.VMEM((rows + 1, width, chan), jnp.float32),
            pltpu.VMEM((2 * H, width, chan), jnp.bfloat16),
            pltpu.SMEM((lines,), jnp.int32),
            pltpu.SMEM((lines * cap,), jnp.int32),
            pltpu.SMEM((lines * cap,), jnp.int32),
            pltpu.SMEM((lines * cap,), jnp.float32),
            pltpu.SemaphoreType.DMA((2 + rows,)),
        ],
        compiler_params=pltpu.CompilerParams(vmem_limit_bytes=56 * 2**20),
        cost_estimate=pl.CostEstimate(flops=0, bytes_accessed=0, transcendentals=0),
        name="backward",
    )(table, cot, weight)


WAITS = (-1, 3)
ADDED = 4
TIED = True


def swap(value, bit, size):
    return lax.ppermute(value, "lat", [(i, i ^ bit) for i in range(size)])


def sum_over_lat(keep, send, between):
    size = lax.axis_size("lat")
    shape = keep.shape
    index = lax.axis_index("lat")
    whole = keep.reshape(-1, shape[-1])
    whole = whole + swap(send.reshape(-1, shape[-1]), 1, size).astype(jnp.float32)
    (whole,) = between(-1, [whole])
    values = list(jnp.split(whole, 2))
    rest = [1 << b for b in range(1, size.bit_length() - 1)]
    orders = [rest[1:] + rest[:1], rest]
    for step in range(len(rest) - 1):
        values = between(step, values)
        for j in range(2):
            bit = orders[j][step]
            side = (index // bit) % 2
            count = values[j].shape[0] // 2
            kept = lax.dynamic_slice_in_dim(values[j], side * count, count, 0)
            sent = lax.dynamic_slice_in_dim(values[j], (1 - side) * count, count, 0)
            got = swap(sent.astype(jnp.bfloat16), bit, size)
            values[j] = kept + got.astype(jnp.float32)
    values = between(len(rest) - 1, values)
    for j in range(2):
        sent = values[j].astype(jnp.bfloat16)
        got = swap(sent, orders[j][-1], size)
        values[j] = (sent.astype(jnp.float32) + got.astype(jnp.float32)).astype(jnp.bfloat16)
    for step in reversed(range(len(rest) - 1)):
        values = between(2 * len(rest) - 2 - step, values)
        for j in range(2):
            bit = orders[j][step]
            side = (index // bit) % 2
            got = swap(values[j], bit, size)
            values[j] = jnp.where(
                side == 0,
                jnp.concatenate([values[j], got]),
                jnp.concatenate([got, values[j]]),
            )
    values = between(2 * len(rest) - 1, values)
    parts = []
    for value in values:
        got = swap(value, 1, size)
        first = jnp.where(index % 2 == 0, value, got)
        second = jnp.where(index % 2 == 0, got, value)
        part = (shape[0] // 2, *shape[1:])
        parts.append(jnp.concatenate([first.reshape(part), second.reshape(part)], axis=-1))
    return jnp.concatenate(parts, axis=1)


def per_device(inputs, cotangent, weight, pat_rows, pat_lons, pat_vals):
    rows = inputs.shape[0]
    width = inputs.shape[1]
    size = lax.axis_size("lat")
    index = lax.axis_index("lat")
    odd = index % 2 == 1
    fast_pairs = [(i, i ^ 1) for i in range(size)]
    slow_pairs = [(i, i + 1 if i % 2 else i - 1) for i in range(1, size - 1)]
    near_pairs = [pair for pair in slow_pairs if min(pair) % 4 == 1]
    far_pairs = [pair for pair in slow_pairs if min(pair) % 4 == 3]
    if rows == H:
        to_slow = to_fast = inputs
    else:
        head, tail = inputs[:H], inputs[rows - H :]
        to_slow, to_fast = jnp.where(odd, tail, head), jnp.where(odd, head, tail)
    far = lax.ppermute(to_slow, "lat", far_pairs)
    part = to_slow[:, :, :HALF]
    near = [lax.ppermute(part, "lat", near_pairs)]
    rest, part = lax.optimization_barrier((to_slow, part))
    near.append(lax.ppermute(rest[:, :, HALF:], "lat", near_pairs))
    fast = lax.ppermute(to_fast, "lat", fast_pairs)
    side = jnp.full((rows, pat_rows.shape[1], 1), odd, jnp.float32)
    table = [
        lax.dynamic_slice_in_dim(part, index * rows, rows, 0).astype(jnp.float32)
        for part in (pat_rows, pat_lons, pat_vals)
    ]
    table = jnp.concatenate([*table, side], axis=-1)
    grad, edge_slow, edge_fast = backward(table, cotangent, weight)
    near[0], far, fast, edge_slow, edge_fast = lax.optimization_barrier(
        (near[0], far, fast, edge_slow, edge_fast)
    )
    partial, *earlier = forward(table, inputs, near[0], far, fast, cotangent, weight, 0)
    partial, edge_slow, edge_fast = lax.optimization_barrier((partial, edge_slow, edge_fast))
    got_far = lax.ppermute(edge_slow, "lat", far_pairs)
    got_near = lax.ppermute(edge_slow, "lat", near_pairs)
    got_fast = lax.ppermute(edge_fast, "lat", fast_pairs)
    mixed, keep, send = forward(table, inputs, near[1], far, fast, cotangent, weight, 1, (partial, *earlier))
    scale = 1.0 / math.sqrt(pat_rows.shape[0] * width)
    got = [got_far, got_near, got_fast]

    def between(step, values):
        nonlocal grad
        for j in range(2):
            if step == WAITS[j] and j == 0:
                values, got[j] = lax.optimization_barrier((values, got[j]))
            elif step == WAITS[j]:
                values = list(values)
                values[1], got[j] = lax.optimization_barrier((values[1], got[j]))
        if step == WAITS[0]:
            values, got[2] = lax.optimization_barrier((values, got[2]))
        if step == ADDED:
            from_slow = got[0].astype(jnp.float32) + got[1].astype(jnp.float32)
            from_fast = got[2].astype(jnp.float32)
            if rows == H:
                grad = grad + from_slow + from_fast
            else:
                grad = grad.at[:H].add(jnp.where(odd, from_fast, from_slow))
                grad = grad.at[rows - H :].add(jnp.where(odd, from_slow, from_fast))
            grad = grad.astype(jnp.bfloat16)
            if TIED:
                values, grad = lax.optimization_barrier((values, grad))
        return list(values)

    total = sum_over_lat(keep, send, between)
    return (mixed, grad, total.astype(jnp.float32) * scale)


def solution(mesh):
    return jax.shard_map(
        per_device,
        mesh=mesh,
        in_specs=(
            P(("group", "lat"), None, None),
            P(("group", "lat"), None, None),
            P(),
            P(),
            P(),
            P(),
        ),
        out_specs=(
            P(("group", "lat"), None, None),
            P(("group", "lat"), None, None),
            P("group", None, None),
        ),
        check_vma=False,
    )
```

```python
import math

import jax
import jax.numpy as jnp
from jax import lax
from jax.experimental import pallas as pl
from jax.experimental.pallas import tpu as pltpu
from jax.sharding import PartitionSpec as P

H = 2
PAD = 16
GROUP = 4
HALF = 128


def entry(table, i, k, e, ne):
    return (
        table[i, k, e].astype(jnp.int32),
        table[i, k, ne + e].astype(jnp.int32),
        table[i, k, 2 * ne + e],
    )


def fwd_kernel(last, table, *refs):
    if last:
        own, near, far, fast, cot, weight, earlier, keep_in, send_in, mixed, keep, send, xf, basis, cott = refs
    else:
        own, near, far, fast, cot, weight, mixed, keep, send, xf, basis, cott = refs
    rows, width, _ = own.shape
    chan = cot.shape[2]
    nk = weight.shape[0]
    ne = table.shape[2] // 3
    odd = table[0, 0, 3 * ne] > 0.5

    def widen(src, r, dst, more=None):
        def part(at, to):
            piece = src[r, at].astype(jnp.float32)
            if more is not None:
                piece = piece + more[r, at].astype(jnp.float32)
            xf[dst, to] = piece

        part(slice(0, width), slice(PAD, PAD + width))
        part(slice(width - PAD, width), slice(0, PAD))
        part(slice(0, PAD), slice(PAD + width, 2 * PAD + width))

    for r in range(H):
        widen(near, r, jnp.where(odd, H + rows, 0) + r, far)
        widen(fast, r, jnp.where(odd, 0, H + rows) + r)
    for r in range(rows):
        widen(own, r, H + r)
        cott[:, r * width : (r + 1) * width] = cot[r].T
    for i in range(rows):

        def per_k(k, carry):
            t = None
            for e in range(ne):
                line, lon, value = entry(table, i, k, e, ne)
                term = value * xf[i + H + line, pl.ds(PAD + lon, width), :]
                t = term if t is None else t + term
            cols = pl.ds(pl.multiple_of(k * HALF, HALF), HALF)
            basis[i * width : (i + 1) * width, cols] = t.astype(jnp.bfloat16)
            return carry

        lax.fori_loop(0, nk, per_k, 0)
    wflat = weight[...].reshape(nk * HALF, chan)
    parts = 3 * rows
    tile = rows * width // parts
    for p in range(parts):
        i, at = divmod(p * tile, width)
        acc = jnp.dot(basis[p * tile : (p + 1) * tile], wflat, preferred_element_type=jnp.float32)
        if last:
            mixed[i, at : at + tile] = (earlier[i, at : at + tile] + acc).astype(jnp.bfloat16)
        else:
            mixed[i, at : at + tile] = acc
    gwt = jnp.dot(cott[...], basis[...], preferred_element_type=jnp.float32)
    dhalf = chan // 2
    at = nk if last else 0
    if last:
        keep[0:nk] = keep_in[...]
        send[0:nk] = send_in[...]
    for k in range(nk):
        mat = gwt[:, k * HALF : (k + 1) * HALF].T
        low, high = mat[:, :dhalf], mat[:, dhalf:]
        keep[at + k] = jnp.where(odd, high, low)
        send[at + k] = jnp.where(odd, low, high).astype(jnp.bfloat16)


def forward(table, own, near, far, fast, cot, weight, h, earlier=()):
    rows, width, chan = cot.shape
    nk = weight.shape[0]
    smem = pl.BlockSpec(memory_space=pltpu.SMEM)
    vmem = pl.BlockSpec(memory_space=pltpu.VMEM)
    last = len(earlier) > 0
    count = nk * (1 + last)
    half = pl.BlockSpec((rows, width, HALF), lambda g: (0, 0, h))
    side = pl.BlockSpec((H, width, HALF), lambda g: (0, 0, h))
    wide = pl.BlockSpec((rows, width, chan), lambda g: (0, 0, 0))
    edge = pl.BlockSpec((H, width, HALF), lambda g: (0, 0, 0))

    def part(blocks):
        return pl.BlockSpec((blocks, HALF, chan // 2), lambda g: (0, 0, 0))

    return pl.pallas_call(
        lambda *refs: fwd_kernel(last, *refs),
        grid=(1,),
        in_specs=[smem]
        + [half, edge, side, side, wide, pl.BlockSpec((nk, HALF, chan), lambda g: (0, h, 0))]
        + ([wide, part(nk), part(nk)] if last else []),
        out_specs=[wide, part(count), part(count)],
        out_shape=[
            jax.ShapeDtypeStruct((rows, width, chan), jnp.bfloat16 if last else jnp.float32),
            jax.ShapeDtypeStruct((count, HALF, chan // 2), jnp.float32),
            jax.ShapeDtypeStruct((count, HALF, chan // 2), jnp.bfloat16),
        ],
        scratch_shapes=[
            pltpu.VMEM((rows + 2 * H, width + 2 * PAD, HALF), jnp.float32),
            pltpu.VMEM((rows * width, nk * HALF), jnp.bfloat16),
            pltpu.VMEM((chan, rows * width), jnp.bfloat16),
        ],
        compiler_params=pltpu.CompilerParams(vmem_limit_bytes=32 * 2**20),
        cost_estimate=pl.CostEstimate(
            flops=0, bytes_accessed=0, transcendentals=0
        ),
        name="forward",
    )(table, own, near, far, fast, cot, weight, *earlier)


def bwd_kernel(table, cin, win, own, *rest):
    edges, scratch = rest[:2], rest[2:]
    db, acc, narrow, cnt, lst_n, lst_o, lst_v, out_sems = scratch
    rows, width, chan = cin.shape
    nk = win.shape[0]
    ne = table.shape[2] // 3
    odd = table[0, 0, 3 * ne] > 0.5
    nh = chan // HALF
    lines = rows + 2 * H
    cap = rows * nk * ne + 2 * GROUP
    for line in range(lines):
        cnt[line] = 0

    for i in range(rows):

        def bin_one(k, carry):
            for e in range(ne):
                row, lon, value = entry(table, i, k, e, ne)
                line = i + H + row
                c = cnt[line]
                lst_n[line * cap + c] = i * nk + k
                lst_o[line * cap + c] = PAD - lon
                lst_v[line * cap + c] = value
                cnt[line] = c + 1
            return carry

        for k in range(nk):
            bin_one(k, 0)
    for line in range(lines):
        c = cnt[line]
        for g in range(2 * GROUP):
            lst_n[line * cap + c + g] = 0
            lst_o[line * cap + c + g] = PAD
            lst_v[line * cap + c + g] = 0.0
    for i in range(rows):
        for k in range(nk):
            n = i * nk + k
            d = lax.dot_general(
                cin[i], win[k], (((1,), (1,)), ((), ())), preferred_element_type=jnp.float32
            )
            for h in range(nh):
                cols = slice(h * HALF, (h + 1) * HALF)
                db[n, h, PAD : PAD + width] = d[:, cols]
                db[n, h, 0:PAD] = d[width - PAD :, cols]
                db[n, h, PAD + width :] = d[0:PAD, cols]

    def terms(t, g, h):
        s = None
        for j in range(GROUP):
            at = t * cap + g * GROUP + j
            x = lst_v[at] * db[lst_n[at], h, pl.ds(lst_o[at], width), :]
            s = x if s is None else s + x
        return s

    def line_sum(t, slot, dst, row):
        groups = jnp.maximum((cnt[t] + GROUP - 1) // GROUP, 2)
        for h in range(nh):
            acc[slot, :, h * HALF : (h + 1) * HALF] = terms(t, 0, h)

        def group(g, carry):
            for h in range(nh):
                cols = slice(h * HALF, (h + 1) * HALF)
                acc[slot, :, cols] = acc[slot, :, cols] + terms(t, g, h)
            return carry

        lax.fori_loop(1, groups - 1, group, 0)
        for h in range(nh):
            cols = slice(h * HALF, (h + 1) * HALF)
            total = acc[slot, :, cols] + terms(t, groups - 1, h)
            dst[row, :, cols] = total.astype(dst.dtype)

    def edge(s, carry):
        top = (s < H) != odd
        line_sum(jnp.where(top, 0, H + rows) + s % H, rows, narrow, s)
        return carry

    lax.fori_loop(0, 2 * H, edge, 0)
    writes = [
        pltpu.make_async_copy(narrow.at[0:H], edges[0], out_sems.at[0]),
        pltpu.make_async_copy(narrow.at[H:], edges[1], out_sems.at[1]),
    ]
    for r in range(rows):
        writes.append(pltpu.make_async_copy(acc.at[r], own.at[r], out_sems.at[2 + r]))
    for write in writes[:2]:
        write.start()
    for r in range(rows):
        line_sum(H + r, r, acc, r)
        writes[2 + r].start()
    for write in writes:
        write.wait()


def backward(table, cot, weight):
    rows, width, chan = cot.shape
    nk = weight.shape[0]
    ne = table.shape[2] // 3
    smem = pl.BlockSpec(memory_space=pltpu.SMEM)
    anym = pl.BlockSpec(memory_space=pl.ANY)
    lines = rows + 2 * H
    cap = rows * nk * ne + 2 * GROUP
    return pl.pallas_call(
        bwd_kernel,
        in_specs=[smem] + [pl.BlockSpec(memory_space=pltpu.VMEM)] * 2,
        out_specs=[anym] * 3,
        out_shape=[
            jax.ShapeDtypeStruct((rows, width, chan), jnp.float32),
        ]
        + [jax.ShapeDtypeStruct((H, width, chan), jnp.bfloat16)] * 2,
        scratch_shapes=[
            pltpu.VMEM((rows * nk, chan // HALF, width + 2 * PAD, HALF), jnp.float32),
            pltpu.VMEM((rows + 1, width, chan), jnp.float32),
            pltpu.VMEM((2 * H, width, chan), jnp.bfloat16),
            pltpu.SMEM((lines,), jnp.int32),
            pltpu.SMEM((lines * cap,), jnp.int32),
            pltpu.SMEM((lines * cap,), jnp.int32),
            pltpu.SMEM((lines * cap,), jnp.float32),
            pltpu.SemaphoreType.DMA((2 + rows,)),
        ],
        compiler_params=pltpu.CompilerParams(vmem_limit_bytes=56 * 2**20),
        cost_estimate=pl.CostEstimate(flops=0, bytes_accessed=0, transcendentals=0),
        name="backward",
    )(table, cot, weight)


WAITS = (-1, 3)
ADDED = 4
TIED = True


def swap(value, bit, size):
    return lax.ppermute(value, "lat", [(i, i ^ bit) for i in range(size)])


def sum_over_lat(keep, send, between):
    size = lax.axis_size("lat")
    shape = keep.shape
    index = lax.axis_index("lat")
    whole = keep.reshape(-1, shape[-1])
    whole = whole + swap(send.reshape(-1, shape[-1]), 1, size).astype(jnp.float32)
    (whole,) = between(-1, [whole])
    values = list(jnp.split(whole, 2))
    rest = [1 << b for b in range(1, size.bit_length() - 1)]
    orders = [rest[1:] + rest[:1], rest]
    for step in range(len(rest) - 1):
        values = between(step, values)
        for j in (1, 0):
            bit = orders[j][step]
            side = (index // bit) % 2
            count = values[j].shape[0] // 2
            kept = lax.dynamic_slice_in_dim(values[j], side * count, count, 0)
            sent = lax.dynamic_slice_in_dim(values[j], (1 - side) * count, count, 0)
            got = swap(sent.astype(jnp.bfloat16), bit, size)
            values[j] = kept + got.astype(jnp.float32)
    values = between(len(rest) - 1, values)
    for j in range(2):
        sent = values[j].astype(jnp.bfloat16)
        got = swap(sent, orders[j][-1], size)
        values[j] = (sent.astype(jnp.float32) + got.astype(jnp.float32)).astype(jnp.bfloat16)
    for step in reversed(range(len(rest) - 1)):
        values = between(2 * len(rest) - 2 - step, values)
        for j in (1, 0):
            bit = orders[j][step]
            side = (index // bit) % 2
            got = swap(values[j], bit, size)
            values[j] = jnp.where(
                side == 0,
                jnp.concatenate([values[j], got]),
                jnp.concatenate([got, values[j]]),
            )
    values = between(2 * len(rest) - 1, values)
    parts = []
    for value in values:
        got = swap(value, 1, size)
        first = jnp.where(index % 2 == 0, value, got)
        second = jnp.where(index % 2 == 0, got, value)
        part = (shape[0] // 2, *shape[1:])
        parts.append(jnp.concatenate([first.reshape(part), second.reshape(part)], axis=-1))
    return jnp.concatenate(parts, axis=1)


def per_device(inputs, cotangent, weight, pat_rows, pat_lons, pat_vals):
    rows = inputs.shape[0]
    width = inputs.shape[1]
    size = lax.axis_size("lat")
    index = lax.axis_index("lat")
    odd = index % 2 == 1
    fast_pairs = [(i, i ^ 1) for i in range(size)]
    slow_pairs = [(i, i + 1 if i % 2 else i - 1) for i in range(1, size - 1)]
    near_pairs = [pair for pair in slow_pairs if min(pair) % 4 == 1]
    far_pairs = [pair for pair in slow_pairs if min(pair) % 4 == 3]
    if rows == H:
        to_slow = to_fast = inputs
    else:
        head, tail = inputs[:H], inputs[rows - H :]
        to_slow, to_fast = jnp.where(odd, tail, head), jnp.where(odd, head, tail)
    far = lax.ppermute(to_slow, "lat", far_pairs)
    part = to_slow[:, :, :HALF]
    near = [lax.ppermute(part, "lat", near_pairs)]
    rest, part = lax.optimization_barrier((to_slow, part))
    near.append(lax.ppermute(rest[:, :, HALF:], "lat", near_pairs))
    fast = lax.ppermute(to_fast, "lat", fast_pairs)
    side = jnp.full((rows, pat_rows.shape[1], 1), odd, jnp.float32)
    table = [
        lax.dynamic_slice_in_dim(part, index * rows, rows, 0).astype(jnp.float32)
        for part in (pat_rows, pat_lons, pat_vals)
    ]
    table = jnp.concatenate([*table, side], axis=-1)
    grad, edge_slow, edge_fast = backward(table, cotangent, weight)
    near[0], far, fast, edge_slow, edge_fast = lax.optimization_barrier(
        (near[0], far, fast, edge_slow, edge_fast)
    )
    partial, *earlier = forward(table, inputs, near[0], far, fast, cotangent, weight, 0)
    partial, edge_slow, edge_fast = lax.optimization_barrier((partial, edge_slow, edge_fast))
    got_far = lax.ppermute(edge_slow, "lat", far_pairs)
    got_near = lax.ppermute(edge_slow, "lat", near_pairs)
    got_fast = lax.ppermute(edge_fast, "lat", fast_pairs)
    mixed, keep, send = forward(table, inputs, near[1], far, fast, cotangent, weight, 1, (partial, *earlier))
    scale = 1.0 / math.sqrt(pat_rows.shape[0] * width)
    got = [got_far, got_near, got_fast]

    def between(step, values):
        nonlocal grad
        for j in range(2):
            if step == WAITS[j] and j == 0:
                values, got[j] = lax.optimization_barrier((values, got[j]))
            elif step == WAITS[j]:
                values = list(values)
                values[1], got[j] = lax.optimization_barrier((values[1], got[j]))
        if step == WAITS[0]:
            values, got[2] = lax.optimization_barrier((values, got[2]))
        if step == ADDED:
            from_slow = got[0].astype(jnp.float32) + got[1].astype(jnp.float32)
            from_fast = got[2].astype(jnp.float32)
            if rows == H:
                grad = grad + from_slow + from_fast
            else:
                grad = grad.at[:H].add(jnp.where(odd, from_fast, from_slow))
                grad = grad.at[rows - H :].add(jnp.where(odd, from_slow, from_fast))
            grad = grad.astype(jnp.bfloat16)
            if TIED:
                values, grad = lax.optimization_barrier((values, grad))
        return list(values)

    total = sum_over_lat(keep, send, between)
    return (mixed, grad, total.astype(jnp.float32) * scale)


def solution(mesh):
    return jax.shard_map(
        per_device,
        mesh=mesh,
        in_specs=(
            P(("group", "lat"), None, None),
            P(("group", "lat"), None, None),
            P(),
            P(),
            P(),
            P(),
        ),
        out_specs=(
            P(("group", "lat"), None, None),
            P(("group", "lat"), None, None),
            P("group", None, None),
        ),
        check_vma=False,
    )
```
